32 devices in a mesh: pipe: 4 (over y, core), dp: 8 (over z, x).
Axes of the slice: x: 2, y: 2, z: 4, core: 2. Of those that a mesh axis runs over, the one named last changes fastest.
Arguments:
- weights: bfloat16 [4, 2, 7168, 256], P('pipe'), may hold values from -0.375 to 0.375
- gain_model: bfloat16 [4, 7168], P('pipe'), may hold values from 0.099609375 to 1.8984375
- gain_latent: bfloat16 [4, 256], P('pipe'), may hold values from 0.099609375 to 1.8984375
- saved_down: bfloat16 [4, 2, 256, 7168], P('pipe', None, 'dp'), may hold values from -6 to 6
- saved_up: bfloat16 [4, 2, 256, 7168], P('pipe', None, 'dp'), may hold values from -6 to 6
- grad_start: bfloat16 [2, 4, 256, 7168], P(None, 'pipe', 'dp'), may hold values from -0.119628906 to 0.119628906
Outputs:
- section_grads: bfloat16 [4, 2, 7168, 256], P('pipe', None, 'dp')
The draws below stay inside these ranges and needn't reach their ends.
All inputs are finite; a program needn't handle non-finite values.
Results may differ from the reference program's by a relative error of at most 0.024.
Values may be sent and summed in bfloat16 or wider, within the bound.
No kernel may reach another device: no remote copies, remote signals or barrier semaphores. Data moves between devices by JAX's collectives and lax.ppermute only.
A program may use at most 128 MiB of HBM per device.

```python
import jax
import jax.numpy as jnp
from jax import lax

D = 7168
LAT = 256
STEPS = 2
SECTIONS = 4
ROWS = 256
N_DP = 8


def block_scale(rng, dims, pieces, least, high):
    def one(axis_at, blocks):
        draws = jax.random.uniform(jax.random.fold_in(jax.random.fold_in(rng, 6), axis_at), (blocks,), jnp.float32, least / len(pieces), high / len(pieces))
        return jnp.repeat(jnp.exp(draws), dims[axis_at] // blocks).reshape((-1,) + (1,) * (len(dims) - axis_at - 1))

    gain = one(*pieces[0])
    for cut in pieces[1:]:
        gain = gain * one(*cut)
    return gain


def centred(key, dims, spread, limit, cuts=(), kind=jnp.bfloat16):
    drawn = spread * jax.random.normal(key, dims, jnp.float32)
    if cuts:
        drawn = drawn * block_scale(key, dims, cuts, -0.22, 0.18)
    return jnp.clip(drawn, -limit, limit).astype(kind)


def setup_inputs(seed: int = 0) -> dict:
    streams_of = jax.random.split(jax.random.key(seed), 7)
    weights = centred(streams_of[0], (SECTIONS, 2, D, LAT), LAT ** -0.5, 0.375, ((0, 4),))
    gain_model = jnp.clip(1.0 + 0.18 * jax.random.normal(streams_of[1], (SECTIONS, D), jnp.float32), 0.099609375, 1.8984375).astype(jnp.bfloat16)
    gain_latent = jnp.clip(1.0 + 0.18 * jax.random.normal(streams_of[2], (SECTIONS, LAT), jnp.float32), 0.099609375, 1.8984375).astype(jnp.bfloat16)
    saved_down = centred(streams_of[3], (SECTIONS, STEPS, ROWS, D), 1.0, 6.0, ((0, 4), (2, 8)))
    saved_up = centred(streams_of[4], (SECTIONS, STEPS, ROWS, D), 1.0, 6.0, ((0, 4), (2, 8)))
    grad_start = centred(streams_of[5], (2, SECTIONS, ROWS, D), 0.02, 0.119628906, ((1, 4), (2, 8)))
    return {"weights": weights, "gain_model": gain_model, "gain_latent": gain_latent, "saved_down": saved_down, "saved_up": saved_up, "grad_start": grad_start}


EPS = 1e-06

def backward(inputs, incoming, pair, gain_in, gain_lat, need_input):
    xf = inputs.astype(jnp.float32)
    inv_in = lax.rsqrt(lax.optimization_barrier(jnp.mean(xf * xf, axis=-1, keepdims=True)) + EPS)
    normed = (xf * inv_in * gain_in.astype(jnp.float32)).astype(jnp.bfloat16)
    latent = jnp.dot(normed, pair[0], preferred_element_type=jnp.float32)
    inv_lat = lax.rsqrt(lax.optimization_barrier(jnp.mean(latent * latent, axis=-1, keepdims=True)) + EPS)
    keyed = (latent * inv_lat * gain_lat.astype(jnp.float32)).astype(jnp.bfloat16)
    dkey = jnp.dot(incoming, pair[1], preferred_element_type=jnp.float32)
    scaled = dkey * gain_lat.astype(jnp.float32)
    dlat = (inv_lat * (scaled - latent * inv_lat * inv_lat * lax.optimization_barrier(jnp.mean(scaled * latent, axis=-1, keepdims=True)))).astype(jnp.bfloat16)
    result = None
    if need_input:
        dnorm = jnp.dot(dlat, pair[0].T, preferred_element_type=jnp.float32)
        vgrad = dnorm * gain_in.astype(jnp.float32)
        result = (incoming.astype(jnp.float32) + inv_in * (vgrad - xf * inv_in * inv_in * lax.optimization_barrier(jnp.mean(vgrad * xf, axis=-1, keepdims=True)))).astype(jnp.bfloat16)
    return (normed, keyed, dlat, result)

def replica_terms(inputs, incoming, pair, gain_in, gain_lat):
    normed, keyed, dlat, unused = backward(inputs, incoming, pair, gain_in, gain_lat, False)
    rows = inputs.shape[0]
    per = rows // N_DP
    normed = normed.reshape(N_DP, per, -1).astype(jnp.float32)
    dlat = dlat.reshape(N_DP, per, -1).astype(jnp.float32)
    keyed = keyed.reshape(N_DP, per, -1).astype(jnp.float32)
    upper = incoming.reshape(N_DP, per, -1).astype(jnp.float32)
    first = jnp.einsum('jti,jtk->jik', normed, dlat)
    second = jnp.einsum('jti,jtk->jik', upper, keyed)
    return jnp.stack([first, second], axis=1)

def reference(weights, gain_model, gain_latent, saved_down, saved_up, grad_start):
    sections = weights.shape[0]
    order = jnp.arange(sections)

    def input_grad(inputs, incoming, section):
        return backward(inputs, incoming, weights[section], gain_model[section], gain_latent[section], True)[3]
    down0 = lax.map(lambda s: input_grad(saved_down[s, 0], grad_start[0, s], s), order)
    up0 = lax.map(lambda r: input_grad(saved_up[r, 0], grad_start[1, r], sections - 1 - r), order)
    zero = jnp.zeros_like(down0[:1])
    down_in = jnp.concatenate([down0[1:], zero], axis=0)
    up_in = jnp.concatenate([zero, up0[:-1]], axis=0)

    def section_grad(s):
        r = sections - 1 - s
        pair = weights[s]
        g_in = gain_model[s]
        g_lat = gain_latent[s]
        down = replica_terms(saved_down[s, 0], grad_start[0, s], pair, g_in, g_lat) + replica_terms(saved_down[s, 1], down_in[s], pair, g_in, g_lat)
        upward = replica_terms(saved_up[r, 0], grad_start[1, r], pair, g_in, g_lat) + replica_terms(saved_up[r, 1], up_in[r], pair, g_in, g_lat)
        down_low = lax.optimization_barrier(down.astype(jnp.bfloat16)).astype(jnp.float32)
        up_low = lax.optimization_barrier(upward.astype(jnp.bfloat16)).astype(jnp.float32)
        total = lax.optimization_barrier(jnp.sum(down_low, axis=0)) + lax.optimization_barrier(jnp.sum(up_low, axis=0))
        return total.astype(jnp.bfloat16)
    return lax.map(section_grad, order)
```

```python
import jax
import jax.numpy as jnp
from jax import lax
from jax.sharding import PartitionSpec as P

EPS = 1e-06


def rows_dot(left, right):
    return lax.dot_general(left, right, (((0,), (0,)), ((), ())), preferred_element_type=jnp.float32)


def dot_t(left, right):
    return lax.dot_general(left, right, (((1,), (1,)), ((), ())), preferred_element_type=jnp.float32)


def dot(left, right):
    return jnp.dot(left, right, preferred_element_type=jnp.float32)


def latent_side(x, down, g, h):
    xf = x.astype(jnp.float32)
    a = lax.rsqrt(jnp.mean(xf * xf, axis=-1, keepdims=True) + EPS)
    c = dot((xf * a * g).astype(jnp.bfloat16), down)
    b = lax.rsqrt(jnp.mean(c * c, axis=-1, keepdims=True) + EPS)
    k = (c * b * h).astype(jnp.bfloat16)
    return a, c, b, k


def gradient_side(y, up, a, c, b, h):
    u = dot(y, up) * h
    q = b * (u - c * b * b * jnp.mean(u * c, axis=-1, keepdims=True))
    return (q * a).astype(jnp.bfloat16)


def input_gradient(x, y, aq, s, down, g):
    return (y.astype(jnp.float32) + dot_t(aq, down) * g - x.astype(jnp.float32) * s).astype(jnp.bfloat16)


def per_device(weights, gain_model, gain_latent, saved_down, saved_up, grad_start):
    ranks = lax.axis_size("pipe")
    replicas = lax.axis_size("dp")
    j = lax.axis_index("dp")
    down, up = weights[0, 0], weights[0, 1]
    width = down.shape[0]
    share = width // replicas
    g = gain_model[0].astype(jnp.float32)
    h = gain_latent[0].astype(jnp.float32)
    own_down = lax.dynamic_slice_in_dim(down, j * share, share, 0)
    own_g = lax.dynamic_slice_in_dim(g, j * share, share, 0)

    def mirror(block):
        return lax.ppermute(block, "pipe", [(i, ranks - 1 - i) for i in range(ranks)])

    def to_before(block):
        return lax.ppermute(block, "pipe", [(i + 1, i) for i in range(ranks - 1)])

    def across(block, apart):
        return lax.ppermute(block, "dp", [(i, i ^ apart) for i in range(replicas)])

    def exchange(blocks):
        out = []
        for apart in range(replicas):
            at = (j ^ apart) * share
            piece = jnp.stack([lax.dynamic_slice_in_dim(b, at, share, 1) for b in blocks])
            out.append(across(piece, apart) if apart else piece)
        return jnp.stack(out, 1)

    def gather(block):
        return jnp.stack([across(block, apart) if apart else block for apart in range(replicas)])

    x0u = mirror(saved_up[0, 0])
    y0u = mirror(grad_start[1, 0])
    x1u = mirror(saved_up[0, 1])
    x0d, x1d, y0d = saved_down[0, 0], saved_down[0, 1], grad_start[0, 0]

    x0d_s, y0d_s = exchange([x0d, y0d])

    def first(x, y):
        a, c, b, k = latent_side(x, down, g, h)
        aq = gradient_side(y, up, a, c, b, h)
        s = a * jnp.sum(aq.astype(jnp.float32) * c, axis=-1, keepdims=True) / width
        z = input_gradient(x, y, aq, s, down, g)
        return aq, k, s, to_before(z)

    def pack(aq, s):
        high = s.astype(jnp.bfloat16)
        low = (s - high.astype(jnp.float32)).astype(jnp.bfloat16)
        pad = jnp.zeros((aq.shape[0], 126), jnp.bfloat16)
        return jnp.concatenate([aq, high, low, pad], 1)

    aq0d, k0d, s0d, y1d = first(x0d, y0d)
    a1d, c1d, b1d, k1d = latent_side(x1d, down, g, h)
    aq1d = gradient_side(y1d, up, a1d, c1d, b1d, h)

    aq0u, k0u, s0u, y1u = first(x0u, y0u)
    x0u_s, y0u_s = exchange([x0u, y0u])
    a1u, c1u, b1u, k1u = latent_side(x1u, down, g, h)
    x1d_s, x1u_s = exchange([x1d, x1u])

    packed = gather(jnp.stack([pack(aq0d, s0d), pack(aq0u, s0u)]))
    aq1u = gradient_side(y1u, up, a1u, c1u, b1u, h)
    late = gather(jnp.stack([jnp.concatenate([k0d, k1d, aq1d], 1), jnp.concatenate([k0u, k1u, aq1u], 1)]))
    lat = h.shape[0]

    x0_s = jnp.stack([x0d_s, x0u_s], 1)
    y0_s = jnp.stack([y0d_s, y0u_s], 1)
    x1_s = jnp.stack([x1d_s, x1u_s], 1)
    flat = lambda v: v.reshape(-1, v.shape[-1])
    x0_s, y0_s, x1_s = flat(x0_s), flat(y0_s), flat(x1_s)
    packed, late = flat(packed), flat(late)
    aq0_all = packed[:, :lat]
    s_all = packed[:, lat : lat + 1].astype(jnp.float32) + packed[:, lat + 1 : lat + 2].astype(jnp.float32)
    k0_all, k1_all, aq1_all = late[:, :lat], late[:, lat : 2 * lat], late[:, 2 * lat :]
    y1_s = to_before(input_gradient(x0_s, y0_s, aq0_all, s_all, own_down, own_g))
    first_term = (rows_dot(x0_s, aq0_all) + rows_dot(x1_s, aq1_all)) * own_g[:, None]
    second_term = rows_dot(y0_s, k0_all) + rows_dot(y1_s, k1_all)
    return jnp.stack([first_term, second_term]).astype(jnp.bfloat16)[None]


def solution(mesh):
    placed = (
        P("pipe", None, None, None),
        P("pipe", None),
        P("pipe", None),
        P("pipe", None, "dp", None),
        P("pipe", None, "dp", None),
        P(None, "pipe", "dp", None),
    )
    return jax.shard_map(
        per_device,
        mesh=mesh,
        in_specs=placed,
        out_specs=P("pipe", None, "dp", None),
        check_vma=False,
    )
```

```python
import functools

import jax
import jax.numpy as jnp
from jax import lax
from jax.experimental import pallas as pl
from jax.experimental.pallas import tpu as pltpu
from jax.sharding import PartitionSpec as P

EPS = 1e-06
LANES = 128
LIMIT = 48 * 1024 * 1024
F32 = jnp.float32
BF16 = jnp.bfloat16


def rows_dot(left, right):
    return lax.dot_general(left, right, (((0,), (0,)), ((), ())), preferred_element_type=F32)


def dot_t(left, right):
    return lax.dot_general(left, right, (((1,), (1,)), ((), ())), preferred_element_type=F32)


def dot(left, right):
    return jnp.dot(left, right, preferred_element_type=F32)


def norm_scale(v):
    return lax.rsqrt(jnp.mean(v * v, axis=-1, keepdims=True) + EPS)


def with_scalar(aq, s):
    high = s.astype(BF16).astype(F32)
    at = lax.broadcasted_iota(jnp.int32, (aq.shape[0], LANES), 1)
    tail = jnp.where(at == 0, high, jnp.where(at == 1, s - high, 0.0)).astype(BF16)
    return jnp.concatenate([aq, tail], 1)


def pack_kernel(parts, share, *refs):
    count = len(refs) - 2
    sources, out, sems = refs[:count], refs[count], refs[count + 1]
    copies = []
    for i, source in enumerate(sources):
        for d in range(parts):
            copies.append(
                pltpu.make_async_copy(
                    source.at[:, pl.ds(d * share, share)], out.at[d, i], sems.at[i * parts + d]
                )
            )
    for copy in copies:
        copy.start()
    for copy in copies:
        copy.wait()


def pack(blocks, parts):
    rows, width = blocks[0].shape
    share = width // parts
    if share % LANES:
        return jnp.stack([b.reshape(rows, parts, share).swapaxes(0, 1) for b in blocks], 1)
    count = len(blocks)
    return pl.pallas_call(
        functools.partial(pack_kernel, parts, share),
        out_shape=jax.ShapeDtypeStruct((parts, count, rows, share), BF16),
        in_specs=[pl.BlockSpec(memory_space=pl.ANY)] * count,
        out_specs=pl.BlockSpec(memory_space=pl.ANY),
        scratch_shapes=[pltpu.SemaphoreType.DMA((count * parts,))],
        name="pack",
    )(*blocks)


CHUNKS = 7


def load_chunks(source, buffer, sems, chunk):
    copies = []
    for i in range(CHUNKS):
        part = pl.ds(i * chunk, chunk)
        copies.append(pltpu.make_async_copy(source.at[part], buffer.at[part], sems.at[i]))
    for copy in copies:
        copy.start()
    return copies


def chunked_dot(left, copies, buffer, chunk):
    total = None
    for i, copy in enumerate(copies):
        copy.wait()
        part = dot(left[:, i * chunk : (i + 1) * chunk], buffer[i * chunk : (i + 1) * chunk, :])
        total = part if total is None else total + part
    return total


def latent_gradient(u, c, a, b):
    q = b * (u - c * b * b * jnp.mean(u * c, axis=-1, keepdims=True))
    return (q * a).astype(BF16)


def first_kernel(with_next, x_ref, y_ref, *rest):
    if with_next:
        x1_ref, w_ref, g_ref, h_ref, z_ref, aq_ref, k_ref, k1_ref, c1_ref, ab1_ref, down, up, sem0, sem1 = rest
    else:
        w_ref, g_ref, h_ref, z_ref, aq_ref, k_ref, down, up, sem0, sem1 = rest
    rows, width = x_ref.shape
    chunk = width // CHUNKS
    copies0 = load_chunks(w_ref.at[0, 0], down, sem0, chunk)
    copies1 = load_chunks(w_ref.at[0, 1], up, sem1, chunk)
    g = g_ref[...].astype(F32)
    h = h_ref[...].astype(F32)
    x = x_ref[...].astype(F32)
    a = norm_scale(x)
    normed = (x * a * g).astype(BF16)
    if with_next:
        x1 = x1_ref[...].astype(F32)
        a1 = norm_scale(x1)
        normed = jnp.concatenate([normed, (x1 * a1 * g).astype(BF16)], 0)
    c = chunked_dot(normed, copies0, down, chunk)
    if with_next:
        c1 = c[rows:]
        c = c[:rows]
        b1 = norm_scale(c1)
        k1_ref[...] = (c1 * b1 * h).astype(BF16)
        c1_ref[...] = c1
        at = lax.broadcasted_iota(jnp.int32, (rows, LANES), 1)
        ab1_ref[...] = jnp.where(at == 0, a1, b1)
    b = norm_scale(c)
    k_ref[...] = (c * b * h).astype(BF16)
    u = chunked_dot(y_ref[...], copies1, up, chunk) * h
    aq = latent_gradient(u, c, a, b)
    s = a * jnp.sum(aq.astype(F32) * c, axis=-1, keepdims=True) / width
    aq_ref[...] = with_scalar(aq, s)
    for i in range(CHUNKS):
        cols = slice(i * chunk, (i + 1) * chunk)
        m = dot_t(aq, down[cols, :])
        z = y_ref[:, cols].astype(F32) + m * g[:, cols] - x_ref[:, cols].astype(F32) * s
        z_ref[:, cols] = z.astype(BF16)


ANY = pl.BlockSpec(memory_space=pl.ANY)
VMEM = pl.BlockSpec(memory_space=pltpu.VMEM)


def shape(*dims, dtype=BF16):
    return jax.ShapeDtypeStruct(dims, dtype)


def first_step(x, y, weights, g, h, x1=None):
    rows, width = x.shape
    lat = h.shape[1]
    outs = [shape(rows, width), shape(rows, lat + LANES), shape(rows, lat)]
    if x1 is not None:
        outs += [shape(rows, lat), shape(rows, lat, dtype=F32), shape(rows, LANES, dtype=F32)]
    wide = [x, y] if x1 is None else [x, y, x1]
    return pl.pallas_call(
        functools.partial(first_kernel, x1 is not None),
        out_shape=outs,
        in_specs=[VMEM] * len(wide) + [ANY, VMEM, VMEM],
        out_specs=[VMEM] * len(outs),
        scratch_shapes=[
            pltpu.VMEM((width, lat), BF16),
            pltpu.VMEM((width, lat), BF16),
            pltpu.SemaphoreType.DMA((CHUNKS,)),
            pltpu.SemaphoreType.DMA((CHUNKS,)),
        ],
        compiler_params=pltpu.CompilerParams(vmem_limit_bytes=LIMIT),
        cost_estimate=pl.CostEstimate(flops=6 * rows * width * lat, bytes_accessed=4 * width * lat + 6 * rows * width, transcendentals=0),
        name="first_step",
    )(*wide, weights, g, h)


def latent_kernel(x_ref, w_ref, g_ref, h_ref, k_ref, c_ref, ab_ref, down, sem):
    rows, width = x_ref.shape
    chunk = width // CHUNKS
    copies = load_chunks(w_ref.at[0, 0], down, sem, chunk)
    h = h_ref[...].astype(F32)
    x = x_ref[...].astype(F32)
    a = norm_scale(x)
    c = chunked_dot((x * a * g_ref[...].astype(F32)).astype(BF16), copies, down, chunk)
    b = norm_scale(c)
    k_ref[...] = (c * b * h).astype(BF16)
    c_ref[...] = c
    at = lax.broadcasted_iota(jnp.int32, (rows, LANES), 1)
    ab_ref[...] = jnp.where(at == 0, a, b)


def latent_side(x, weights, g, h):
    rows, width = x.shape
    lat = h.shape[1]
    outs = [shape(rows, lat), shape(rows, lat, dtype=F32), shape(rows, LANES, dtype=F32)]
    return pl.pallas_call(
        latent_kernel,
        out_shape=outs,
        in_specs=[VMEM, ANY, VMEM, VMEM],
        out_specs=[VMEM] * 3,
        scratch_shapes=[pltpu.VMEM((width, lat), BF16), pltpu.SemaphoreType.DMA((CHUNKS,))],
        compiler_params=pltpu.CompilerParams(vmem_limit_bytes=LIMIT),
        cost_estimate=pl.CostEstimate(flops=2 * rows * width * lat, bytes_accessed=2 * width * lat + 2 * rows * width, transcendentals=0),
        name="latent_side",
    )(x, weights, g, h)


def second_kernel(y0_ref, y1_ref, w_ref, h_ref, c0_ref, c1_ref, ab0_ref, ab1_ref, aq_ref, up, sem):
    rows, width = y0_ref.shape
    chunk = width // CHUNKS
    copies = load_chunks(w_ref.at[0, 1], up, sem, chunk)
    y = jnp.concatenate([y0_ref[...], y1_ref[...]], 0)
    u = chunked_dot(y, copies, up, chunk) * h_ref[...].astype(F32)
    aq_ref[:rows] = latent_gradient(u[:rows], c0_ref[...], ab0_ref[:, 0:1], ab0_ref[:, 1:2])
    aq_ref[rows:] = latent_gradient(u[rows:], c1_ref[...], ab1_ref[:, 0:1], ab1_ref[:, 1:2])


def second_step(y0, y1, weights, h, c0, c1, ab0, ab1):
    rows, width = y0.shape
    lat = h.shape[1]
    return pl.pallas_call(
        second_kernel,
        out_shape=shape(2 * rows, lat),
        in_specs=[VMEM, VMEM, ANY, VMEM, VMEM, VMEM, VMEM, VMEM],
        out_specs=VMEM,
        scratch_shapes=[pltpu.VMEM((width, lat), BF16), pltpu.SemaphoreType.DMA((CHUNKS,))],
        compiler_params=pltpu.CompilerParams(vmem_limit_bytes=LIMIT),
        cost_estimate=pl.CostEstimate(flops=4 * rows * width * lat, bytes_accessed=2 * width * lat + 4 * rows * width, transcendentals=0),
        name="second_step",
    )(y0, y1, weights, h, c0, c1, ab0, ab1)


def columns_kernel(lat, d_ref, u_ref, aq_ref, down_ref, g_ref, z_ref):
    parts, two, rows, share = d_ref.shape
    g = g_ref[...].astype(F32)
    down = down_ref[...]
    for i, ref in enumerate((d_ref, u_ref)):
        narrow = aq_ref[:, i * rows : (i + 1) * rows, :].reshape(parts * rows, lat + LANES)
        s = narrow[:, lat : lat + 1].astype(F32) + narrow[:, lat + 1 : lat + 2].astype(F32)
        m = dot_t(narrow[:, :lat], down)
        x = ref[:, 0].reshape(parts * rows, share).astype(F32)
        y = ref[:, 1].reshape(parts * rows, share).astype(F32)
        z_ref[i] = (y + m * g - x * s).astype(BF16)


def columns_step(d, u, aq, down, g):
    parts, two, rows, share = d.shape
    lat = down.shape[1]
    return pl.pallas_call(
        functools.partial(columns_kernel, lat),
        out_shape=shape(2, parts * rows, share),
        in_specs=[VMEM] * 5,
        out_specs=VMEM,
        compiler_params=pltpu.CompilerParams(vmem_limit_bytes=LIMIT),
        cost_estimate=pl.CostEstimate(flops=4 * parts * rows * share * lat, bytes_accessed=12 * parts * rows * share, transcendentals=0),
        name="columns_step",
    )(d, u, aq, down, g)


def terms_kernel(d_ref, u_ref, x1_ref, y1_ref, aq0_ref, aq1_ref, k_ref, g_ref, out_ref):
    parts, two, rows, share = d_ref.shape
    lat = aq1_ref.shape[2]
    total = parts * rows

    def half(ref, i, start=0):
        return ref[:, i * rows : (i + 1) * rows, start : start + lat].reshape(total, lat)

    def wide(ref, i):
        return ref[:, i].reshape(total, share)

    first = rows_dot(wide(d_ref, 0), half(aq0_ref, 0))
    first += rows_dot(wide(u_ref, 0), half(aq0_ref, 1))
    first += rows_dot(wide(x1_ref, 0), half(aq1_ref, 0))
    first += rows_dot(wide(x1_ref, 1), half(aq1_ref, 1))
    out_ref[0, 0] = (first * g_ref[...].astype(F32)).astype(BF16)
    second = rows_dot(wide(d_ref, 1), half(k_ref, 0))
    second += rows_dot(wide(u_ref, 1), half(k_ref, 1))
    second += rows_dot(y1_ref[0], half(k_ref, 0, lat))
    second += rows_dot(y1_ref[1], half(k_ref, 1, lat))
    out_ref[0, 1] = second.astype(BF16)


def terms(d, u, x1, y1, aq0, aq1, k, g):
    parts, two, rows, share = d.shape
    lat = aq1.shape[2]
    return pl.pallas_call(
        terms_kernel,
        out_shape=shape(1, 2, share, lat),
        in_specs=[VMEM] * 8,
        out_specs=VMEM,
        compiler_params=pltpu.CompilerParams(vmem_limit_bytes=LIMIT),
        cost_estimate=pl.CostEstimate(flops=16 * parts * rows * share * lat, bytes_accessed=16 * parts * rows * share, transcendentals=0),
        name="terms",
    )(d, u, x1, y1, aq0, aq1, k, g)


def per_device(weights, gain_model, gain_latent, saved_down, saved_up, grad_start):
    ranks = lax.axis_size("pipe")
    replicas = lax.axis_size("dp")
    j = lax.axis_index("dp")
    share = weights.shape[2] // replicas
    own_down = lax.dynamic_slice_in_dim(weights[0, 0], j * share, share, 0)
    own_g = lax.dynamic_slice_in_dim(gain_model, j * share, share, 1)

    def mirror(block):
        return lax.ppermute(block, "pipe", [(i, ranks - 1 - i) for i in range(ranks)])

    def to_before(block):
        return lax.ppermute(block, "pipe", [(i + 1, i) for i in range(ranks - 1)])

    def exchange(blocks):
        return lax.all_to_all(pack(blocks, replicas), "dp", 0, 0, tiled=True)

    def spread(block):
        return lax.all_to_all(jnp.broadcast_to(block[None], (replicas,) + block.shape), "dp", 0, 0, tiled=True)

    x0u = mirror(saved_up[0, 0])
    y0u = mirror(grad_start[1, 0])
    x1u = mirror(saved_up[0, 1])
    x0d, x1d, y0d = saved_down[0, 0], saved_down[0, 1], grad_start[0, 0]

    d_s = exchange([x0d, y0d])
    z0d, aq0d, k0d, k1d, c1d, ab1d = first_step(x0d, y0d, weights, gain_model, gain_latent, x1d)
    y1d = to_before(z0d)
    z0u, aq0u, k0u = first_step(x0u, y0u, weights, gain_model, gain_latent)
    y1u = to_before(z0u)
    u_s = exchange([x0u, y0u])
    aq0 = spread(jnp.concatenate([aq0d, aq0u], 0))
    k1u, c1u, ab1u = latent_side(x1u, weights, gain_model, gain_latent)
    k = lax.all_gather(jnp.concatenate([jnp.concatenate([k0d, k1d], 1), jnp.concatenate([k0u, k1u], 1)], 0), "dp")
    aq1 = spread(second_step(y1d, y1u, weights, gain_latent, c1d, c1u, ab1d, ab1u))
    x1_s = exchange([x1d, x1u])
    y1_s = to_before(columns_step(d_s, u_s, aq0, own_down, own_g))
    return terms(d_s, u_s, x1_s, y1_s, aq0, aq1, k, own_g.reshape(share, 1))


def solution(mesh):
    placed = (
        P("pipe", None, None, None),
        P("pipe", None),
        P("pipe", None),
        P("pipe", None, "dp", None),
        P("pipe", None, "dp", None),
        P(None, "pipe", "dp", None),
    )
    return jax.shard_map(
        per_device,
        mesh=mesh,
        in_specs=placed,
        out_specs=P("pipe", None, "dp", None),
        check_vma=False,
    )
```

```python
import functools

import jax
import jax.numpy as jnp
from jax import lax
from jax.experimental import pallas as pl
from jax.experimental.pallas import tpu as pltpu
from jax.sharding import PartitionSpec as P

EPS = 1e-06
LANES = 128
ANY = pl.BlockSpec(memory_space=pl.ANY)
VMEM = pl.BlockSpec(memory_space=pltpu.VMEM)
SMEM = pl.BlockSpec(memory_space=pltpu.SMEM)
LIMIT = 48 * 1024 * 1024
F32 = jnp.float32
BF16 = jnp.bfloat16


def rows_dot(left, right):
    return lax.dot_general(left, right, (((0,), (0,)), ((), ())), preferred_element_type=F32)


def dot_t(left, right):
    return lax.dot_general(left, right, (((1,), (1,)), ((), ())), preferred_element_type=F32)


def dot(left, right):
    return jnp.dot(left, right, preferred_element_type=F32)


def norm_scale(v):
    return lax.rsqrt(jnp.mean(v * v, axis=-1, keepdims=True) + EPS)


def with_scalar(aq, s):
    high = s.astype(BF16).astype(F32)
    at = lax.broadcasted_iota(jnp.int32, (aq.shape[0], LANES), 1)
    tail = jnp.where(at == 0, high, jnp.where(at == 1, s - high, 0.0)).astype(BF16)
    return jnp.concatenate([aq, tail], 1)


def pack_kernel(parts, share, *refs):
    out = refs[-1]
    for i, source in enumerate(refs[:-1]):
        for d in range(parts):
            out[d, i] = source[:, d * share : (d + 1) * share]


def pack(blocks, parts):
    rows, width = blocks[0].shape
    share = width // parts
    count = len(blocks)
    return pl.pallas_call(
        functools.partial(pack_kernel, parts, share),
        out_shape=jax.ShapeDtypeStruct((parts, count, rows, share), BF16),
        in_specs=[VMEM] * count,
        out_specs=VMEM,
        compiler_params=pltpu.CompilerParams(vmem_limit_bytes=LIMIT),
        cost_estimate=pl.CostEstimate(flops=0, bytes_accessed=4 * count * rows * width, transcendentals=0),
        name="pack",
    )(*blocks)


CHUNKS = 7


def load_chunks(source, buffer, sems, chunk):
    copies = []
    for i in range(CHUNKS):
        part = pl.ds(i * chunk, chunk)
        copies.append(pltpu.make_async_copy(source.at[part], buffer.at[part], sems.at[i]))
    for copy in copies:
        copy.start()
    return copies


def chunked_dot(left, copies, buffer, chunk):
    total = None
    for i, copy in enumerate(copies):
        copy.wait()
        part = dot(left[:, i * chunk : (i + 1) * chunk], buffer[i * chunk : (i + 1) * chunk, :])
        total = part if total is None else total + part
    return total


def latent_gradient(u, c, a, b):
    q = b * (u - c * b * b * jnp.mean(u * c, axis=-1, keepdims=True))
    return (q * a).astype(BF16)


def first_kernel(with_next, x_ref, y_ref, *rest):
    if with_next:
        x1_ref, w_ref, g_ref, h_ref, z_ref, narrow_ref, k1_ref, c1_ref, ab1_ref, down, up, sem0, sem1 = rest
    else:
        before_ref, w_ref, g_ref, h_ref, z_ref, narrow_ref, down, up, sem0, sem1 = rest
    rows, width = x_ref.shape
    lat = h_ref.shape[1]
    chunk = width // CHUNKS
    copies0 = load_chunks(w_ref.at[0, 0], down, sem0, chunk)
    copies1 = load_chunks(w_ref.at[0, 1], up, sem1, chunk)
    g = g_ref[...].astype(F32)
    h = h_ref[...].astype(F32)
    x = x_ref[...].astype(F32)
    a = norm_scale(x)
    normed = (x * a * g).astype(BF16)
    if with_next:
        x1 = x1_ref[...].astype(F32)
        a1 = norm_scale(x1)
        normed = jnp.concatenate([normed, (x1 * a1 * g).astype(BF16)], 0)
    c = chunked_dot(normed, copies0, down, chunk)
    mine = slice(0, rows)
    if with_next:
        c1 = c[rows:]
        c = c[:rows]
        b1 = norm_scale(c1)
        k1_ref[...] = (c1 * b1 * h).astype(BF16)
        c1_ref[...] = c1
        at = lax.broadcasted_iota(jnp.int32, (rows, LANES), 1)
        ab1_ref[...] = jnp.where(at == 0, a1, b1)
    else:
        narrow_ref[:rows] = before_ref[...]
        mine = slice(rows, 2 * rows)
    b = norm_scale(c)
    narrow_ref[mine, lat + LANES :] = (c * b * h).astype(BF16)
    u = chunked_dot(y_ref[...], copies1, up, chunk) * h
    aq = latent_gradient(u, c, a, b)
    s = a * jnp.sum(aq.astype(F32) * c, axis=-1, keepdims=True) / width
    narrow_ref[mine, : lat + LANES] = with_scalar(aq, s)
    for i in range(CHUNKS):
        cols = slice(i * chunk, (i + 1) * chunk)
        m = dot_t(aq, down[cols, :])
        z = y_ref[:, cols].astype(F32) + m * g[:, cols] - x_ref[:, cols].astype(F32) * s
        z_ref[:, cols] = z.astype(BF16)


def shape(*dims, dtype=BF16):
    return jax.ShapeDtypeStruct(dims, dtype)


def first_step(x, y, weights, g, h, x1=None, before=None):
    rows, width = x.shape
    lat = h.shape[1]
    narrow = 2 * lat + LANES
    if before is None:
        outs = [shape(rows, width), shape(rows, narrow), shape(rows, lat), shape(rows, lat, dtype=F32), shape(rows, LANES, dtype=F32)]
        wide = [x, y, x1]
    else:
        outs = [shape(rows, width), shape(2 * rows, narrow)]
        wide = [x, y, before]
    return pl.pallas_call(
        functools.partial(first_kernel, before is None),
        out_shape=outs,
        in_specs=[VMEM] * len(wide) + [ANY, VMEM, VMEM],
        out_specs=[VMEM] * len(outs),
        scratch_shapes=[
            pltpu.VMEM((width, lat), BF16),
            pltpu.VMEM((width, lat), BF16),
            pltpu.SemaphoreType.DMA((CHUNKS,)),
            pltpu.SemaphoreType.DMA((CHUNKS,)),
        ],
        compiler_params=pltpu.CompilerParams(vmem_limit_bytes=LIMIT),
        cost_estimate=pl.CostEstimate(flops=6 * rows * width * lat, bytes_accessed=4 * width * lat + 6 * rows * width, transcendentals=0),
        name="first_step",
    )(*wide, weights, g, h)


def latent_kernel(x_ref, w_ref, g_ref, h_ref, k_ref, c_ref, ab_ref, down, sem):
    rows, width = x_ref.shape
    chunk = width // CHUNKS
    copies = load_chunks(w_ref.at[0, 0], down, sem, chunk)
    h = h_ref[...].astype(F32)
    x = x_ref[...].astype(F32)
    a = norm_scale(x)
    c = chunked_dot((x * a * g_ref[...].astype(F32)).astype(BF16), copies, down, chunk)
    b = norm_scale(c)
    k_ref[...] = (c * b * h).astype(BF16)
    c_ref[...] = c
    at = lax.broadcasted_iota(jnp.int32, (rows, LANES), 1)
    ab_ref[...] = jnp.where(at == 0, a, b)


def latent_side(x, weights, g, h):
    rows, width = x.shape
    lat = h.shape[1]
    outs = [shape(rows, lat), shape(rows, lat, dtype=F32), shape(rows, LANES, dtype=F32)]
    return pl.pallas_call(
        latent_kernel,
        out_shape=outs,
        in_specs=[VMEM, ANY, VMEM, VMEM],
        out_specs=[VMEM] * 3,
        scratch_shapes=[pltpu.VMEM((width, lat), BF16), pltpu.SemaphoreType.DMA((CHUNKS,))],
        compiler_params=pltpu.CompilerParams(vmem_limit_bytes=LIMIT),
        cost_estimate=pl.CostEstimate(flops=2 * rows * width * lat, bytes_accessed=2 * width * lat + 2 * rows * width, transcendentals=0),
        name="latent_side",
    )(x, weights, g, h)


def second_kernel(y0_ref, y1_ref, w_ref, h_ref, c0_ref, c1_ref, ab0_ref, ab1_ref, k0_ref, k1_ref, out_ref, up, sem):
    rows, width = y0_ref.shape
    lat = h_ref.shape[1]
    chunk = width // CHUNKS
    copies = load_chunks(w_ref.at[0, 1], up, sem, chunk)
    out_ref[:rows, lat:] = k0_ref[...]
    out_ref[rows:, lat:] = k1_ref[...]
    y = jnp.concatenate([y0_ref[...], y1_ref[...]], 0)
    u = chunked_dot(y, copies, up, chunk) * h_ref[...].astype(F32)
    out_ref[:rows, :lat] = latent_gradient(u[:rows], c0_ref[...], ab0_ref[:, 0:1], ab0_ref[:, 1:2])
    out_ref[rows:, :lat] = latent_gradient(u[rows:], c1_ref[...], ab1_ref[:, 0:1], ab1_ref[:, 1:2])


def second_step(y0, y1, weights, h, c0, c1, ab0, ab1, k0, k1):
    rows, width = y0.shape
    lat = h.shape[1]
    return pl.pallas_call(
        second_kernel,
        out_shape=shape(2 * rows, 2 * lat),
        in_specs=[VMEM, VMEM, ANY] + [VMEM] * 7,
        out_specs=VMEM,
        scratch_shapes=[pltpu.VMEM((width, lat), BF16), pltpu.SemaphoreType.DMA((CHUNKS,))],
        compiler_params=pltpu.CompilerParams(vmem_limit_bytes=LIMIT),
        cost_estimate=pl.CostEstimate(flops=4 * rows * width * lat, bytes_accessed=2 * width * lat + 4 * rows * width, transcendentals=0),
        name="second_step",
    )(y0, y1, weights, h, c0, c1, ab0, ab1, k0, k1)


def far_bits(parts):
    bits, at = [], parts // 2
    while at:
        bits.append(at)
        at //= 2
    return bits


def held_order(parts):
    order = [0]
    for bit in far_bits(parts):
        order += [p ^ bit for p in order]
    return order


def gather_pieces(block, axis):
    parts = lax.axis_size(axis)
    pieces, held = [block], block
    for bit in far_bits(parts):
        pieces.append(lax.ppermute(held, axis, [(i, i ^ bit) for i in range(parts)]))
        if bit > 1:
            held = jnp.concatenate([held, pieces[-1]], 0)
    return pieces


def restore(j, pieces, out):
    parts, rows = out.shape[:2]
    order, at = held_order(parts), 0
    for piece in pieces:
        for i in range(piece.shape[0] // rows):
            out[j ^ order[at]] = piece[i * rows : (i + 1) * rows, :]
            at += 1


def columns_kernel(lat, j_ref, d_ref, u_ref, down_ref, g_ref, *rest):
    pieces, z_ref, narrow_ref = rest[:-2], rest[-2], rest[-1]
    parts, two, rows, share = d_ref.shape
    restore(j_ref[0], pieces, narrow_ref)
    g = g_ref[...].astype(F32)
    down = down_ref[...]
    for i, ref in enumerate((d_ref, u_ref)):
        narrow = narrow_ref[:, i * rows : (i + 1) * rows, :].reshape(parts * rows, narrow_ref.shape[2])
        s = narrow[:, lat : lat + 1].astype(F32) + narrow[:, lat + 1 : lat + 2].astype(F32)
        m = dot_t(narrow[:, :lat], down)
        x = ref[:, 0].reshape(parts * rows, share).astype(F32)
        y = ref[:, 1].reshape(parts * rows, share).astype(F32)
        z_ref[i] = (y + m * g - x * s).astype(BF16)


def columns_step(j, d, u, down, g, pieces):
    parts, two, rows, share = d.shape
    lat = down.shape[1]
    narrow = pieces[0].shape
    return pl.pallas_call(
        functools.partial(columns_kernel, lat),
        out_shape=[shape(2, parts * rows, share), shape(parts, *narrow)],
        in_specs=[SMEM] + [VMEM] * (4 + len(pieces)),
        out_specs=[VMEM, VMEM],
        compiler_params=pltpu.CompilerParams(vmem_limit_bytes=LIMIT),
        cost_estimate=pl.CostEstimate(flops=4 * parts * rows * share * lat, bytes_accessed=12 * parts * rows * share, transcendentals=0),
        name="columns_step",
    )(j, d, u, down, g, *pieces)


def terms_kernel(j_ref, d_ref, u_ref, x1_ref, y1_ref, first_ref, g_ref, *rest):
    pieces, out_ref, second_ref = rest[:-2], rest[-2], rest[-1]
    parts, two, rows, share = d_ref.shape
    lat = second_ref.shape[2] // 2
    total = parts * rows
    restore(j_ref[0], pieces, second_ref)

    def half(ref, i, start):
        return ref[:, i * rows : (i + 1) * rows, start : start + lat].reshape(total, lat)

    def wide(ref, i):
        return ref[:, i].reshape(total, share)

    first = rows_dot(wide(d_ref, 0), half(first_ref, 0, 0))
    first += rows_dot(wide(u_ref, 0), half(first_ref, 1, 0))
    first += rows_dot(wide(x1_ref, 0), half(second_ref, 0, 0))
    first += rows_dot(wide(x1_ref, 1), half(second_ref, 1, 0))
    out_ref[0, 0] = (first * g_ref[...].astype(F32)).astype(BF16)
    second = rows_dot(wide(d_ref, 1), half(first_ref, 0, lat + LANES))
    second += rows_dot(wide(u_ref, 1), half(first_ref, 1, lat + LANES))
    second += rows_dot(y1_ref[0], half(second_ref, 0, lat))
    second += rows_dot(y1_ref[1], half(second_ref, 1, lat))
    out_ref[0, 1] = second.astype(BF16)


def terms(j, d, u, x1, y1, first, g, pieces):
    parts, two, rows, share = d.shape
    narrow = pieces[0].shape
    lat = narrow[1] // 2
    return pl.pallas_call(
        terms_kernel,
        out_shape=shape(1, 2, share, lat),
        in_specs=[SMEM] + [VMEM] * (6 + len(pieces)),
        out_specs=VMEM,
        scratch_shapes=[pltpu.VMEM((parts,) + narrow, BF16)],
        compiler_params=pltpu.CompilerParams(vmem_limit_bytes=LIMIT),
        cost_estimate=pl.CostEstimate(flops=16 * parts * rows * share * lat, bytes_accessed=16 * parts * rows * share, transcendentals=0),
        name="terms",
    )(j, d, u, x1, y1, first, g, *pieces)


def per_device(weights, gain_model, gain_latent, saved_down, saved_up, grad_start):
    ranks = lax.axis_size("pipe")
    replicas = lax.axis_size("dp")
    j = lax.axis_index("dp")
    share = weights.shape[2] // replicas
    own_down = lax.dynamic_slice_in_dim(weights[0, 0], j * share, share, 0)
    own_g = lax.dynamic_slice_in_dim(gain_model, j * share, share, 1)

    def mirror(block):
        return lax.ppermute(block, "pipe", [(i, ranks - 1 - i) for i in range(ranks)])

    def to_before(block):
        return lax.ppermute(block, "pipe", [(i + 1, i) for i in range(ranks - 1)])

    def exchange(blocks):
        return lax.all_to_all(blocks, "dp", 0, 0, tiled=True)

    x0u = mirror(saved_up[0, 0])
    y0u = mirror(grad_start[1, 0])
    x1u = mirror(saved_up[0, 1])
    x0d, x1d, y0d = saved_down[0, 0], saved_down[0, 1], grad_start[0, 0]

    d_packed, x0d, y0d, x1d = lax.optimization_barrier((pack([x0d, y0d], replicas), x0d, y0d, x1d))
    d_s = exchange(d_packed)
    z0d, before, k1d, c1d, ab1d = first_step(x0d, y0d, weights, gain_model, gain_latent, x1d)
    y1d = to_before(z0d)
    u_packed, x0u, y0u = lax.optimization_barrier((pack([x0u, y0u], replicas), x0u, y0u))
    u_s = exchange(u_packed)
    z0u, narrow = first_step(x0u, y0u, weights, gain_model, gain_latent, before=before)
    y1u = to_before(z0u)
    first_pieces = gather_pieces(narrow, "dp")
    k1u, c1u, ab1u = latent_side(x1u, weights, gain_model, gain_latent)
    second = second_step(y1d, y1u, weights, gain_latent, c1d, c1u, ab1d, ab1u, k1d, k1u)
    x1_s = exchange(pack([x1d, x1u], replicas))
    second_pieces = gather_pieces(second, "dp")
    z0_s, first = columns_step(j[None], d_s, u_s, own_down, own_g, first_pieces)
    y1_s = to_before(z0_s)
    return terms(j[None], d_s, u_s, x1_s, y1_s, first, own_g.reshape(share, 1), second_pieces)


def solution(mesh):
    placed = (
        P("pipe", None, None, None),
        P("pipe", None),
        P("pipe", None),
        P("pipe", None, "dp", None),
        P("pipe", None, "dp", None),
        P(None, "pipe", "dp", None),
    )
    return jax.shard_map(
        per_device,
        mesh=mesh,
        in_specs=placed,
        out_specs=P("pipe", None, "dp", None),
        check_vma=False,
    )
```

```python
import functools

import jax
import jax.numpy as jnp
from jax import lax
from jax.experimental import pallas as pl
from jax.experimental.pallas import tpu as pltpu
from jax.sharding import PartitionSpec as P

EPS = 1e-06
LANES = 128
ANY = pl.BlockSpec(memory_space=pl.ANY)
VMEM = pl.BlockSpec(memory_space=pltpu.VMEM)
SMEM = pl.BlockSpec(memory_space=pltpu.SMEM)
LIMIT = 62 * 1024 * 1024
COST = pl.CostEstimate(flops=1, bytes_accessed=1, transcendentals=0)
F32 = jnp.float32
BF16 = jnp.bfloat16


def rows_dot(left, right):
    return lax.dot_general(left, right, (((0,), (0,)), ((), ())), preferred_element_type=F32)


def dot_t(left, right):
    return lax.dot_general(left, right, (((1,), (1,)), ((), ())), preferred_element_type=F32)


def dot(left, right):
    return jnp.dot(left, right, preferred_element_type=F32)


def norm_scale(v):
    return lax.rsqrt(jnp.mean(v * v, axis=-1, keepdims=True) + EPS)


def with_scalar(aq, s):
    high = s.astype(BF16).astype(F32)
    at = lax.broadcasted_iota(jnp.int32, (aq.shape[0], LANES), 1)
    tail = jnp.where(at == 0, high, jnp.where(at == 1, s - high, 0.0)).astype(BF16)
    return jnp.concatenate([aq, tail], 1)


def pack_into(out, sources):
    parts, share = out.shape[0], out.shape[3]
    for i, source in enumerate(sources):
        for d in range(parts):
            out[d, i] = source[:, d * share : (d + 1) * share]


def pack_kernel(*refs):
    pack_into(refs[-1], refs[:-1])


def pack(blocks, parts):
    rows, width = blocks[0].shape
    count = len(blocks)
    return pl.pallas_call(
        pack_kernel,
        out_shape=shape(parts, count, rows, width // parts),
        in_specs=[VMEM] * count,
        out_specs=VMEM,
        compiler_params=pltpu.CompilerParams(vmem_limit_bytes=LIMIT),
        cost_estimate=COST,
        name="pack",
    )(*blocks)


def run_copies(pairs, sems):
    copies = [pltpu.make_async_copy(source, target, sems.at[i]) for i, (source, target) in enumerate(pairs)]
    for copy in copies:
        copy.start()
    for copy in copies:
        copy.wait()


def prepare_kernel(down_ref, up_ref, start_ref, packed_ref, x0_ref, y0_ref, x1_ref, sems):
    parts, three, rows, share = packed_ref.shape
    pairs = []
    for i, source in enumerate((down_ref.at[0, 0], start_ref.at[0, 0], down_ref.at[0, 1])):
        for d in range(parts):
            pairs.append((source.at[:, pl.ds(d * share, share)], packed_ref.at[d, i]))
    pairs += [(up_ref.at[0, 0], x0_ref), (start_ref.at[1, 0], y0_ref), (up_ref.at[0, 1], x1_ref)]
    run_copies(pairs, sems)


def prepare(saved_down, saved_up, grad_start, parts):
    rows, width = saved_down.shape[2:]
    share = width // parts
    if share % LANES:
        x0, y0, x1 = saved_up[0, 0], grad_start[1, 0], saved_up[0, 1]
        return pack([saved_down[0, 0], grad_start[0, 0], saved_down[0, 1]], parts), x0, y0, x1
    return pl.pallas_call(
        prepare_kernel,
        out_shape=[shape(parts, 3, rows, share)] + [shape(rows, width)] * 3,
        in_specs=[ANY] * 3,
        out_specs=[VMEM] * 4,
        scratch_shapes=[pltpu.SemaphoreType.DMA((3 * parts + 3,))],
        compiler_params=pltpu.CompilerParams(vmem_limit_bytes=LIMIT),
        cost_estimate=COST,
        name="prepare",
    )(saved_down, saved_up, grad_start)


def shape(*dims, dtype=BF16):
    return jax.ShapeDtypeStruct(dims, dtype)


CHUNKS = 4


def load_chunks(source, buffer, sems):
    chunk = buffer.shape[0] // CHUNKS
    copies = []
    for i in range(CHUNKS):
        part = pl.ds(i * chunk, chunk)
        copies.append(pltpu.make_async_copy(source.at[part], buffer.at[part], sems.at[i]))
    for copy in copies:
        copy.start()
    return copies


def chunked_dot(left, copies, buffer):
    chunk = buffer.shape[0] // CHUNKS
    total = None
    for i, copy in enumerate(copies):
        copy.wait()
        part = dot(left[:, i * chunk : (i + 1) * chunk], buffer[i * chunk : (i + 1) * chunk, :])
        total = part if total is None else total + part
    return total


def latent_gradient(u, c, a, b):
    q = b * (u - c * b * b * jnp.mean(u * c, axis=-1, keepdims=True))
    return (q * a).astype(BF16)


def next_latent(c, a, h, k_ref, c_ref, ab_ref):
    b = norm_scale(c)
    k_ref[...] = (c * b * h).astype(BF16)
    c_ref[...] = c
    at = lax.broadcasted_iota(jnp.int32, (c.shape[0], LANES), 1)
    ab_ref[...] = jnp.where(at == 0, a, b)


def first_kernel(stacked, x_ref, y_ref, w_ref, g_ref, h_ref, *rest):
    rest, (down, up, sem0, sem1) = rest[:-4], rest[-4:]
    copies0 = load_chunks(w_ref.at[0, 0], down, sem0)
    copies1 = load_chunks(w_ref.at[0, 1], up, sem1)
    if stacked:
        x_ref, x1_ref, y_ref = x_ref.at[0, 0], x_ref.at[0, 1], y_ref.at[0, 0]
        z_ref, narrow_ref, k1_ref, c1_ref, ab1_ref = rest
        mine = slice(0, x_ref.shape[0])
    else:
        before_ref, z_ref, narrow_ref = rest
        narrow_ref[: x_ref.shape[0]] = before_ref[...]
        mine = slice(x_ref.shape[0], 2 * x_ref.shape[0])
    rows, width = x_ref.shape
    lat = h_ref.shape[1]
    chunk = width // CHUNKS
    g = g_ref[...].astype(F32)
    h = h_ref[...].astype(F32)
    x = x_ref[...].astype(F32)
    a = norm_scale(x)
    normed = (x * a * g).astype(BF16)
    if stacked:
        x1 = x1_ref[...].astype(F32)
        a1 = norm_scale(x1)
        normed = jnp.concatenate([normed, (x1 * a1 * g).astype(BF16)], 0)
    c = chunked_dot(normed, copies0, down)
    u = chunked_dot(y_ref[...], copies1, up) * h
    if stacked:
        c1 = c[rows:]
        c = c[:rows]
        next_latent(c1, a1, h, k1_ref, c1_ref, ab1_ref)
    b = norm_scale(c)
    narrow_ref[mine, lat + LANES :] = (c * b * h).astype(BF16)
    aq = latent_gradient(u, c, a, b)
    s = a * jnp.sum(aq.astype(F32) * c, axis=-1, keepdims=True) / width
    narrow_ref[mine, : lat + LANES] = with_scalar(aq, s)
    for i in range(CHUNKS):
        cols = slice(i * chunk, (i + 1) * chunk)
        m = dot_t(aq, down[cols, :])
        z = y_ref[:, cols].astype(F32) + m * g[:, cols] - x_ref[:, cols].astype(F32) * s
        z_ref[:, cols] = z.astype(BF16)


def first_step(x, y, weights, g, h, before=None):
    rows, width = x.shape[-2:]
    lat = h.shape[1]
    operands = [x, y, weights, g, h]
    outs = [shape(rows, width)]
    if before is None:
        outs += [shape(rows, 2 * lat + LANES), shape(rows, lat), shape(rows, lat, dtype=F32), shape(rows, LANES, dtype=F32)]
    else:
        outs += [shape(2 * rows, 2 * lat + LANES)]
        operands += [before]
    return pl.pallas_call(
        functools.partial(first_kernel, before is None),
        out_shape=outs,
        in_specs=[VMEM] * 2 + [ANY] + [VMEM] * (len(operands) - 3),
        out_specs=[VMEM] * len(outs),
        scratch_shapes=[pltpu.VMEM((width, lat), BF16)] * 2 + [pltpu.SemaphoreType.DMA((CHUNKS,))] * 2,
        compiler_params=pltpu.CompilerParams(vmem_limit_bytes=LIMIT),
        cost_estimate=COST,
        name="first_step",
    )(*operands)


def latent_kernel(x_ref, w_ref, g_ref, h_ref, k_ref, c_ref, ab_ref, down, sem):
    copies = load_chunks(w_ref.at[0, 0], down, sem)
    x = x_ref[...].astype(F32)
    a = norm_scale(x)
    c = chunked_dot((x * a * g_ref[...].astype(F32)).astype(BF16), copies, down)
    next_latent(c, a, h_ref[...].astype(F32), k_ref, c_ref, ab_ref)


def latent_side(x, weights, g, h):
    rows, width = x.shape
    lat = h.shape[1]
    outs = [shape(rows, lat), shape(rows, lat, dtype=F32), shape(rows, LANES, dtype=F32)]
    return pl.pallas_call(
        latent_kernel,
        out_shape=outs,
        in_specs=[VMEM, ANY, VMEM, VMEM],
        out_specs=[VMEM] * 3,
        scratch_shapes=[pltpu.VMEM((width, lat), BF16), pltpu.SemaphoreType.DMA((CHUNKS,))],
        compiler_params=pltpu.CompilerParams(vmem_limit_bytes=LIMIT),
        cost_estimate=COST,
        name="latent_side",
    )(x, weights, g, h)


def gradient_kernel(x_ref, y_ref, w_ref, g_ref, h_ref, k_ref, c_ref, ab_ref, before_ref, z_ref, narrow_ref, down, up, sem0, sem1):
    copies1 = load_chunks(w_ref.at[0, 1], up, sem1)
    copies0 = load_chunks(w_ref.at[0, 0], down, sem0)
    rows, width = x_ref.shape
    lat = h_ref.shape[1]
    chunk = width // CHUNKS
    c, a, b = c_ref[...], ab_ref[:, 0:1], ab_ref[:, 1:2]
    narrow_ref[:rows] = before_ref[...]
    narrow_ref[rows:, lat + LANES :] = k_ref[...]
    aq = latent_gradient(chunked_dot(y_ref[...], copies1, up) * h_ref[...].astype(F32), c, a, b)
    s = a * jnp.sum(aq.astype(F32) * c, axis=-1, keepdims=True) / width
    narrow_ref[rows:, : lat + LANES] = with_scalar(aq, s)
    for i, copy in enumerate(copies0):
        copy.wait()
        cols = slice(i * chunk, (i + 1) * chunk)
        m = dot_t(aq, down[cols, :])
        z = y_ref[:, cols].astype(F32) + m * g_ref[:, cols].astype(F32) - x_ref[:, cols].astype(F32) * s
        z_ref[:, cols] = z.astype(BF16)


def gradient_step(x, y, weights, g, h, k, c, ab, before):
    rows, width = x.shape
    lat = h.shape[1]
    return pl.pallas_call(
        gradient_kernel,
        out_shape=[shape(rows, width), shape(2 * rows, 2 * lat + LANES)],
        in_specs=[VMEM] * 2 + [ANY] + [VMEM] * 6,
        out_specs=[VMEM] * 2,
        scratch_shapes=[pltpu.VMEM((width, lat), BF16)] * 2 + [pltpu.SemaphoreType.DMA((CHUNKS,))] * 2,
        compiler_params=pltpu.CompilerParams(vmem_limit_bytes=LIMIT),
        cost_estimate=COST,
        name="gradient_step",
    )(x, y, weights, g, h, k, c, ab, before)


def second_kernel(y0_ref, y1_ref, w_ref, h_ref, c0_ref, c1_ref, ab0_ref, ab1_ref, k0_ref, k1_ref, out_ref, up, sem):
    copies = load_chunks(w_ref.at[0, 1], up, sem)
    rows, width = y0_ref.shape
    lat = h_ref.shape[1]
    out_ref[:rows, lat:] = k0_ref[...]
    out_ref[rows:, lat:] = k1_ref[...]
    y = jnp.concatenate([y0_ref[...], y1_ref[...]], 0)
    u = chunked_dot(y, copies, up) * h_ref[...].astype(F32)
    out_ref[:rows, :lat] = latent_gradient(u[:rows], c0_ref[...], ab0_ref[:, 0:1], ab0_ref[:, 1:2])
    out_ref[rows:, :lat] = latent_gradient(u[rows:], c1_ref[...], ab1_ref[:, 0:1], ab1_ref[:, 1:2])


def second_step(y0, y1, weights, h, c0, c1, ab0, ab1, k0, k1):
    rows, width = y0.shape
    lat = h.shape[1]
    return pl.pallas_call(
        second_kernel,
        out_shape=shape(2 * rows, 2 * lat),
        in_specs=[VMEM] * 2 + [ANY] + [VMEM] * 7,
        out_specs=VMEM,
        scratch_shapes=[pltpu.VMEM((width, lat), BF16), pltpu.SemaphoreType.DMA((CHUNKS,))],
        compiler_params=pltpu.CompilerParams(vmem_limit_bytes=LIMIT),
        cost_estimate=COST,
        name="second_step",
    )(y0, y1, weights, h, c0, c1, ab0, ab1, k0, k1)


def held_order(parts):
    far = list(range(parts - 2, 0, -2))
    return [0] + far + [p ^ 1 for p in [0] + far]


def gather_pieces(block, axis):
    parts = lax.axis_size(axis)

    def across(held, apart):
        return lax.ppermute(held, axis, [(i, i ^ apart) for i in range(parts)])

    pieces = [block] + [across(block, apart) for apart in range(parts - 2, 0, -2)]
    return pieces + [across(jnp.concatenate(pieces, 0), 1)]


def restore(j, pieces, out):
    parts, rows = out.shape[:2]
    order, at = held_order(parts), 0
    for piece in pieces:
        for i in range(piece.shape[0] // rows):
            out[j ^ order[at]] = piece[i * rows : (i + 1) * rows, :]
            at += 1


def columns_of(x, y, narrow, down, g):
    parts, rows, share = x.shape
    lat = down.shape[3]
    narrow = narrow.reshape(parts * rows, narrow.shape[2])
    s = narrow[:, lat : lat + 1].astype(F32) + narrow[:, lat + 1 : lat + 2].astype(F32)
    m = dot_t(narrow[:, :lat], down[0, 0])
    x = x.reshape(parts * rows, share).astype(F32)
    y = y.reshape(parts * rows, share).astype(F32)
    return (y + m * g[...].astype(F32) - x * s).astype(BF16)


def columns_first_kernel(j_ref, d_ref, down_ref, g_ref, *rest):
    pieces, z_ref, narrow_ref = rest[:-2], rest[-2], rest[-1]
    restore(j_ref[0], pieces, narrow_ref)
    rows = d_ref.shape[2]
    z_ref[...] = columns_of(d_ref[:, 0], d_ref[:, 1], narrow_ref[:, :rows, :], down_ref, g_ref)


def columns_next_kernel(u_ref, down_ref, g_ref, narrow_ref, z_ref):
    rows = u_ref.shape[2]
    z_ref[...] = columns_of(u_ref[:, 0], u_ref[:, 1], narrow_ref[:, rows:, :], down_ref, g_ref)


def columns_first(j, d, down, g, pieces):
    parts, two, rows, share = d.shape
    lat = down.shape[3]
    return pl.pallas_call(
        columns_first_kernel,
        out_shape=[shape(parts * rows, share), shape(parts, *pieces[0].shape)],
        in_specs=[SMEM] + [VMEM] * (3 + len(pieces)),
        out_specs=[VMEM, VMEM],
        compiler_params=pltpu.CompilerParams(vmem_limit_bytes=LIMIT),
        cost_estimate=COST,
        name="columns_first",
    )(j, d, down, g, *pieces)


def columns_next(u, down, g, narrow):
    parts, two, rows, share = u.shape
    lat = down.shape[3]
    return pl.pallas_call(
        columns_next_kernel,
        out_shape=shape(parts * rows, share),
        in_specs=[VMEM] * 4,
        out_specs=VMEM,
        compiler_params=pltpu.CompilerParams(vmem_limit_bytes=LIMIT),
        cost_estimate=COST,
        name="columns_next",
    )(u, down, g, narrow)


def terms_kernel(j_ref, d_ref, u_ref, y1d_ref, y1u_ref, first_ref, g_ref, *rest):
    pieces, out_ref, second_ref = rest[:-2], rest[-2], rest[-1]
    parts, two, rows, share = d_ref.shape
    lat = second_ref.shape[2] // 2
    total = parts * rows
    restore(j_ref[0], pieces, second_ref)

    def half(ref, i, start):
        return ref[:, i * rows : (i + 1) * rows, start : start + lat].reshape(total, lat)

    def wide(ref, i):
        return ref[:, i].reshape(total, share)

    first = rows_dot(wide(d_ref, 0), half(first_ref, 0, 0))
    first += rows_dot(wide(u_ref, 0), half(first_ref, 1, 0))
    first += rows_dot(wide(d_ref, 2), half(second_ref, 0, 0))
    first += rows_dot(wide(u_ref, 2), half(second_ref, 1, 0))
    out_ref[0, 0] = (first * g_ref[...].astype(F32)).astype(BF16)
    second = rows_dot(wide(d_ref, 1), half(first_ref, 0, lat + LANES))
    second += rows_dot(wide(u_ref, 1), half(first_ref, 1, lat + LANES))
    second += rows_dot(y1d_ref[...], half(second_ref, 0, lat))
    second += rows_dot(y1u_ref[...], half(second_ref, 1, lat))
    out_ref[0, 1] = second.astype(BF16)


def terms(j, d, u, y1d, y1u, first, g, pieces):
    parts, two, rows, share = d.shape
    narrow = pieces[0].shape
    lat = narrow[1] // 2
    return pl.pallas_call(
        terms_kernel,
        out_shape=shape(1, 2, share, lat),
        in_specs=[SMEM] + [VMEM] * (6 + len(pieces)),
        out_specs=VMEM,
        scratch_shapes=[pltpu.VMEM((parts,) + narrow, BF16)],
        compiler_params=pltpu.CompilerParams(vmem_limit_bytes=LIMIT),
        cost_estimate=COST,
        name="terms",
    )(j, d, u, y1d, y1u, first, g, *pieces)


def per_device(weights, gain_model, gain_latent, saved_down, saved_up, grad_start):
    ranks = lax.axis_size("pipe")
    replicas = lax.axis_size("dp")
    j = lax.axis_index("dp")
    share = weights.shape[2] // replicas
    own_down = lax.dynamic_slice(weights, (0, 0, j * share, 0), (1, 1, share, weights.shape[3]))
    own_g = lax.dynamic_slice_in_dim(gain_model, j * share, share, 1)

    def mirror(block):
        return lax.ppermute(block, "pipe", [(i, ranks - 1 - i) for i in range(ranks)])

    def to_before(block):
        return lax.ppermute(block, "pipe", [(i + 1, i) for i in range(ranks - 1)])

    def exchange(blocks):
        return lax.all_to_all(blocks, "dp", 0, 0, tiled=True)

    packed, x0u, y0u, x1u = prepare(saved_down, saved_up, grad_start, replicas)
    packed, x0u, y0u, x1u, saved_down, grad_start = lax.optimization_barrier((packed, x0u, y0u, x1u, saved_down, grad_start))
    x0u, y0u, x1u = mirror(x0u), mirror(y0u), mirror(x1u)
    d_s = exchange(packed)
    z0d, before, k1d, c1d, ab1d = first_step(saved_down, grad_start, weights, gain_model, gain_latent)
    y1d = to_before(z0d)
    x0u, before = lax.optimization_barrier((x0u, before))
    k0u, c0u, ab0u = latent_side(x0u, weights, gain_model, gain_latent)
    y0u, c0u = lax.optimization_barrier((y0u, c0u))
    z0u, narrow = gradient_step(x0u, y0u, weights, gain_model, gain_latent, k0u, c0u, ab0u, before)
    z0u, narrow, y1d = lax.optimization_barrier((z0u, narrow, y1d))
    y1u = to_before(z0u)
    first_pieces = gather_pieces(narrow, "dp")
    far = len(first_pieces) - 1
    u_packed = pack([x0u, y0u, x1u], replicas)
    u_packed, y1u, x1u, d_s, *first_pieces[1:far] = lax.optimization_barrier((u_packed, y1u, x1u, d_s, *first_pieces[1:far]))
    u_s = exchange(u_packed)
    k1u, c1u, ab1u = latent_side(x1u, weights, gain_model, gain_latent)
    second = second_step(y1d, y1u, weights, gain_latent, c1d, c1u, ab1d, ab1u, k1d, k1u)
    second_pieces = gather_pieces(second, "dp")
    z0d_s, first = columns_first(j[None], d_s, own_down, own_g, first_pieces)
    y1d_s = to_before(z0d_s)
    u_s, first, *second_pieces[1:far] = lax.optimization_barrier((u_s, first, *second_pieces[1:far]))
    y1u_s = to_before(columns_next(u_s, own_down, own_g, first))
    return terms(j[None], d_s, u_s, y1d_s, y1u_s, first, own_g.reshape(share, 1), second_pieces)


def solution(mesh):
    placed = (
        P("pipe", None, None, None),
        P("pipe", None),
        P("pipe", None),
        P("pipe", None, "dp", None),
        P("pipe", None, "dp", None),
        P(None, "pipe", "dp", None),
    )
    return jax.shard_map(
        per_device,
        mesh=mesh,
        in_specs=placed,
        out_specs=P("pipe", None, "dp", None),
        check_vma=False,
    )
```

```python
import functools

import jax
import jax.numpy as jnp
from jax import lax
from jax.experimental import pallas as pl
from jax.experimental.pallas import tpu as pltpu
from jax.sharding import PartitionSpec as P

EPS = 1e-06
LANES = 128
ANY = pl.BlockSpec(memory_space=pl.ANY)
VMEM = pl.BlockSpec(memory_space=pltpu.VMEM)
SMEM = pl.BlockSpec(memory_space=pltpu.SMEM)
LIMIT = 62 * 1024 * 1024
LATE = 32 * 1024 * 1024
COST = pl.CostEstimate(flops=1, bytes_accessed=1, transcendentals=0)
F32 = jnp.float32
BF16 = jnp.bfloat16


def rows_dot(left, right):
    return lax.dot_general(left, right, (((0,), (0,)), ((), ())), preferred_element_type=F32)


def dot_t(left, right):
    return lax.dot_general(left, right, (((1,), (1,)), ((), ())), preferred_element_type=F32)


def dot(left, right):
    return jnp.dot(left, right, preferred_element_type=F32)


def norm_scale(v):
    return lax.rsqrt(jnp.mean(v * v, axis=-1, keepdims=True) + EPS)


def with_scalar(aq, s):
    high = s.astype(BF16).astype(F32)
    at = lax.broadcasted_iota(jnp.int32, (aq.shape[0], LANES), 1)
    tail = jnp.where(at == 0, high, jnp.where(at == 1, s - high, 0.0)).astype(BF16)
    return jnp.concatenate([aq, tail], 1)


def pack_into(out, sources):
    parts, share = out.shape[0], out.shape[3]
    for i, source in enumerate(sources):
        for d in range(parts):
            out[d, i] = source[:, d * share : (d + 1) * share]


def pack_kernel(*refs):
    pack_into(refs[-1], refs[:-1])


def pack(blocks, parts):
    rows, width = blocks[0].shape
    count = len(blocks)
    return pl.pallas_call(
        pack_kernel,
        out_shape=shape(parts, count, rows, width // parts),
        in_specs=[VMEM] * count,
        out_specs=VMEM,
        compiler_params=pltpu.CompilerParams(vmem_limit_bytes=LIMIT),
        cost_estimate=COST,
        name="pack",
    )(*blocks)


def run_copies(pairs, sems):
    copies = [pltpu.make_async_copy(source, target, sems.at[i]) for i, (source, target) in enumerate(pairs)]
    for copy in copies:
        copy.start()
    for copy in copies:
        copy.wait()


def prepare_kernel(down_ref, up_ref, start_ref, packed_ref, x0_ref, y0_ref, x1_ref, sems):
    parts, three, rows, share = packed_ref.shape
    pairs = []
    for i, source in enumerate((down_ref.at[0, 0], start_ref.at[0, 0], down_ref.at[0, 1])):
        for d in range(parts):
            pairs.append((source.at[:, pl.ds(d * share, share)], packed_ref.at[d, i]))
    pairs += [(up_ref.at[0, 0], x0_ref), (start_ref.at[1, 0], y0_ref), (up_ref.at[0, 1], x1_ref)]
    run_copies(pairs, sems)


def prepare(saved_down, saved_up, grad_start, parts):
    rows, width = saved_down.shape[2:]
    share = width // parts
    if share % LANES:
        x0, y0, x1 = saved_up[0, 0], grad_start[1, 0], saved_up[0, 1]
        return pack([saved_down[0, 0], grad_start[0, 0], saved_down[0, 1]], parts), x0, y0, x1
    return pl.pallas_call(
        prepare_kernel,
        out_shape=[shape(parts, 3, rows, share)] + [shape(rows, width)] * 3,
        in_specs=[ANY] * 3,
        out_specs=[VMEM] * 4,
        scratch_shapes=[pltpu.SemaphoreType.DMA((3 * parts + 3,))],
        compiler_params=pltpu.CompilerParams(vmem_limit_bytes=LIMIT),
        cost_estimate=COST,
        name="prepare",
    )(saved_down, saved_up, grad_start)


def shape(*dims, dtype=BF16):
    return jax.ShapeDtypeStruct(dims, dtype)


CHUNKS = 4


def load_chunks(source, buffer, sems):
    chunk = buffer.shape[0] // CHUNKS
    copies = []
    for i in range(CHUNKS):
        part = pl.ds(i * chunk, chunk)
        copies.append(pltpu.make_async_copy(source.at[part], buffer.at[part], sems.at[i]))
    for copy in copies:
        copy.start()
    return copies


def chunked_dot(left, copies, buffer):
    chunk = buffer.shape[0] // CHUNKS
    total = None
    for i, copy in enumerate(copies):
        copy.wait()
        part = dot(left[:, i * chunk : (i + 1) * chunk], buffer[i * chunk : (i + 1) * chunk, :])
        total = part if total is None else total + part
    return total


def latent_gradient(u, c, a, b):
    q = b * (u - c * b * b * jnp.mean(u * c, axis=-1, keepdims=True))
    return (q * a).astype(BF16)


def next_latent(c, a, h, k_ref, c_ref, ab_ref):
    b = norm_scale(c)
    k_ref[...] = (c * b * h).astype(BF16)
    c_ref[...] = c
    at = lax.broadcasted_iota(jnp.int32, (c.shape[0], LANES), 1)
    ab_ref[...] = jnp.where(at == 0, a, b)


def first_kernel(stacked, x_ref, y_ref, w_ref, g_ref, h_ref, *rest):
    rest, (down, up, sem0, sem1) = rest[:-4], rest[-4:]
    copies0 = load_chunks(w_ref.at[0, 0], down, sem0)
    copies1 = load_chunks(w_ref.at[0, 1], up, sem1)
    if stacked:
        x_ref, x1_ref, y_ref = x_ref.at[0, 0], x_ref.at[0, 1], y_ref.at[0, 0]
        z_ref, narrow_ref, k1_ref, c1_ref, ab1_ref = rest
        mine = slice(0, x_ref.shape[0])
    else:
        before_ref, z_ref, narrow_ref = rest
        narrow_ref[: x_ref.shape[0]] = before_ref[...]
        mine = slice(x_ref.shape[0], 2 * x_ref.shape[0])
    rows, width = x_ref.shape
    lat = h_ref.shape[1]
    chunk = width // CHUNKS
    g = g_ref[...].astype(F32)
    h = h_ref[...].astype(F32)
    x = x_ref[...].astype(F32)
    a = norm_scale(x)
    normed = (x * a * g).astype(BF16)
    if stacked:
        x1 = x1_ref[...].astype(F32)
        a1 = norm_scale(x1)
        normed = jnp.concatenate([normed, (x1 * a1 * g).astype(BF16)], 0)
    c = chunked_dot(normed, copies0, down)
    u = chunked_dot(y_ref[...], copies1, up) * h
    if stacked:
        c1 = c[rows:]
        c = c[:rows]
        next_latent(c1, a1, h, k1_ref, c1_ref, ab1_ref)
    b = norm_scale(c)
    narrow_ref[mine, lat + LANES :] = (c * b * h).astype(BF16)
    aq = latent_gradient(u, c, a, b)
    s = a * jnp.sum(aq.astype(F32) * c, axis=-1, keepdims=True) / width
    narrow_ref[mine, : lat + LANES] = with_scalar(aq, s)
    for i in range(CHUNKS):
        cols = slice(i * chunk, (i + 1) * chunk)
        m = dot_t(aq, down[cols, :])
        z = y_ref[:, cols].astype(F32) + m * g[:, cols] - x_ref[:, cols].astype(F32) * s
        z_ref[:, cols] = z.astype(BF16)


def first_step(x, y, weights, g, h, before=None):
    rows, width = x.shape[-2:]
    lat = h.shape[1]
    operands = [x, y, weights, g, h]
    outs = [shape(rows, width)]
    if before is None:
        outs += [shape(rows, 2 * lat + LANES), shape(rows, lat), shape(rows, lat, dtype=F32), shape(rows, LANES, dtype=F32)]
    else:
        outs += [shape(2 * rows, 2 * lat + LANES)]
        operands += [before]
    return pl.pallas_call(
        functools.partial(first_kernel, before is None),
        out_shape=outs,
        in_specs=[VMEM] * 2 + [ANY] + [VMEM] * (len(operands) - 3),
        out_specs=[VMEM] * len(outs),
        scratch_shapes=[pltpu.VMEM((width, lat), BF16)] * 2 + [pltpu.SemaphoreType.DMA((CHUNKS,))] * 2,
        compiler_params=pltpu.CompilerParams(vmem_limit_bytes=LIMIT),
        cost_estimate=COST,
        name="first_step",
    )(*operands)


def latent_kernel(x_ref, w_ref, g_ref, h_ref, k_ref, c_ref, ab_ref, down, sem):
    copies = load_chunks(w_ref.at[0, 0], down, sem)
    x = x_ref[...].astype(F32)
    a = norm_scale(x)
    c = chunked_dot((x * a * g_ref[...].astype(F32)).astype(BF16), copies, down)
    next_latent(c, a, h_ref[...].astype(F32), k_ref, c_ref, ab_ref)


def latent_side(x, weights, g, h):
    rows, width = x.shape
    lat = h.shape[1]
    outs = [shape(rows, lat), shape(rows, lat, dtype=F32), shape(rows, LANES, dtype=F32)]
    return pl.pallas_call(
        latent_kernel,
        out_shape=outs,
        in_specs=[VMEM, ANY, VMEM, VMEM],
        out_specs=[VMEM] * 3,
        scratch_shapes=[pltpu.VMEM((width, lat), BF16), pltpu.SemaphoreType.DMA((CHUNKS,))],
        compiler_params=pltpu.CompilerParams(vmem_limit_bytes=LIMIT),
        cost_estimate=COST,
        name="latent_side",
    )(x, weights, g, h)


def narrow_kernel(y_ref, w_ref, h_ref, k_ref, c_ref, ab_ref, before_ref, narrow_ref, up, sem):
    copies = load_chunks(w_ref.at[0, 1], up, sem)
    rows, width = y_ref.shape
    lat = h_ref.shape[1]
    c, a, b = c_ref[...], ab_ref[:, 0:1], ab_ref[:, 1:2]
    narrow_ref[:rows] = before_ref[...]
    narrow_ref[rows:, lat + LANES :] = k_ref[...]
    aq = latent_gradient(chunked_dot(y_ref[...], copies, up) * h_ref[...].astype(F32), c, a, b)
    s = a * jnp.sum(aq.astype(F32) * c, axis=-1, keepdims=True) / width
    narrow_ref[rows:, : lat + LANES] = with_scalar(aq, s)


def narrow_step(y, weights, h, k, c, ab, before):
    rows, width = y.shape
    lat = h.shape[1]
    return pl.pallas_call(
        narrow_kernel,
        out_shape=shape(2 * rows, 2 * lat + LANES),
        in_specs=[VMEM, ANY] + [VMEM] * 5,
        out_specs=VMEM,
        scratch_shapes=[pltpu.VMEM((width, lat), BF16), pltpu.SemaphoreType.DMA((CHUNKS,))],
        compiler_params=pltpu.CompilerParams(vmem_limit_bytes=LIMIT),
        cost_estimate=COST,
        name="narrow_step",
    )(y, weights, h, k, c, ab, before)


def input_kernel(x_ref, y_ref, w_ref, g_ref, narrow_ref, z_ref, packed_ref, down, sem):
    copies = load_chunks(w_ref.at[0, 0], down, sem)
    rows, width = x_ref.shape
    lat = down.shape[1]
    chunk = width // CHUNKS
    pack_into(packed_ref, [x_ref, y_ref])
    aq = narrow_ref[rows:, :lat]
    s = narrow_ref[rows:, lat : lat + 1].astype(F32) + narrow_ref[rows:, lat + 1 : lat + 2].astype(F32)
    for i, copy in enumerate(copies):
        copy.wait()
        cols = slice(i * chunk, (i + 1) * chunk)
        m = dot_t(aq, down[cols, :])
        z = y_ref[:, cols].astype(F32) + m * g_ref[:, cols].astype(F32) - x_ref[:, cols].astype(F32) * s
        z_ref[:, cols] = z.astype(BF16)


def input_step(x, y, weights, g, narrow, parts):
    rows, width = x.shape
    lat = weights.shape[3]
    return pl.pallas_call(
        input_kernel,
        out_shape=[shape(rows, width), shape(parts, 2, rows, width // parts)],
        in_specs=[VMEM] * 2 + [ANY] + [VMEM] * 2,
        out_specs=[VMEM] * 2,
        scratch_shapes=[pltpu.VMEM((width, lat), BF16), pltpu.SemaphoreType.DMA((CHUNKS,))],
        compiler_params=pltpu.CompilerParams(vmem_limit_bytes=LIMIT),
        cost_estimate=COST,
        name="input_step",
    )(x, y, weights, g, narrow)


def second_kernel(x_ref, y0_ref, y1_ref, w_ref, g_ref, h_ref, c0_ref, ab0_ref, k0_ref, out_ref, packed_ref, down, up, sem0, sem1):
    copies0 = load_chunks(w_ref.at[0, 0], down, sem0)
    copies1 = load_chunks(w_ref.at[0, 1], up, sem1)
    rows, width = x_ref.shape
    lat = h_ref.shape[1]
    pack_into(packed_ref, [x_ref])
    h = h_ref[...].astype(F32)
    x = x_ref[...].astype(F32)
    a = norm_scale(x)
    c = chunked_dot((x * a * g_ref[...].astype(F32)).astype(BF16), copies0, down)
    b = norm_scale(c)
    out_ref[:rows, lat:] = k0_ref[...]
    out_ref[rows:, lat:] = (c * b * h).astype(BF16)
    u = chunked_dot(jnp.concatenate([y0_ref[...], y1_ref[...]], 0), copies1, up) * h
    out_ref[:rows, :lat] = latent_gradient(u[:rows], c0_ref[...], ab0_ref[:, 0:1], ab0_ref[:, 1:2])
    out_ref[rows:, :lat] = latent_gradient(u[rows:], c, a, b)


def second_step(x, y0, y1, weights, g, h, c0, ab0, k0, parts):
    rows, width = x.shape
    lat = h.shape[1]
    return pl.pallas_call(
        second_kernel,
        out_shape=[shape(2 * rows, 2 * lat), shape(parts, 1, rows, width // parts)],
        in_specs=[VMEM] * 3 + [ANY] + [VMEM] * 5,
        out_specs=[VMEM] * 2,
        scratch_shapes=[pltpu.VMEM((width, lat), BF16)] * 2 + [pltpu.SemaphoreType.DMA((CHUNKS,))] * 2,
        compiler_params=pltpu.CompilerParams(vmem_limit_bytes=LIMIT),
        cost_estimate=COST,
        name="second_step",
    )(x, y0, y1, weights, g, h, c0, ab0, k0)


def held_order(parts):
    far = list(range(parts - 2, 0, -2))
    return [0] + far + [p ^ 1 for p in [0] + far]


def gather_pieces(block, axis):
    parts = lax.axis_size(axis)

    def across(held, apart):
        return lax.ppermute(held, axis, [(i, i ^ apart) for i in range(parts)])

    pieces = [block] + [across(block, apart) for apart in range(parts - 2, 0, -2)]
    return pieces + [across(jnp.concatenate(pieces, 0), 1)]


def restore(j, pieces, out):
    parts, rows = out.shape[:2]
    order, at = held_order(parts), 0
    for piece in pieces:
        for i in range(piece.shape[0] // rows):
            out[j ^ order[at]] = piece[i * rows : (i + 1) * rows, :]
            at += 1


def columns_of(x, y, narrow, down, g):
    parts, rows, share = x.shape
    lat = down.shape[3]
    narrow = narrow.reshape(parts * rows, narrow.shape[2])
    s = narrow[:, lat : lat + 1].astype(F32) + narrow[:, lat + 1 : lat + 2].astype(F32)
    m = dot_t(narrow[:, :lat], down[0, 0])
    x = x.reshape(parts * rows, share).astype(F32)
    y = y.reshape(parts * rows, share).astype(F32)
    return (y + m * g[...].astype(F32) - x * s).astype(BF16)


def columns_first_kernel(j_ref, d_ref, down_ref, g_ref, *rest):
    pieces, z_ref, narrow_ref = rest[:-2], rest[-2], rest[-1]
    restore(j_ref[0], pieces, narrow_ref)
    rows = d_ref.shape[2]
    z_ref[...] = columns_of(d_ref[:, 0], d_ref[:, 1], narrow_ref[:, :rows, :], down_ref, g_ref)


def columns_next_kernel(u_ref, down_ref, g_ref, narrow_ref, z_ref):
    rows = u_ref.shape[2]
    z_ref[...] = columns_of(u_ref[:, 0], u_ref[:, 1], narrow_ref[:, rows:, :], down_ref, g_ref)


def columns_first(j, d, down, g, pieces):
    parts, two, rows, share = d.shape
    lat = down.shape[3]
    return pl.pallas_call(
        columns_first_kernel,
        out_shape=[shape(parts * rows, share), shape(parts, *pieces[0].shape)],
        in_specs=[SMEM] + [VMEM] * (3 + len(pieces)),
        out_specs=[VMEM, VMEM],
        compiler_params=pltpu.CompilerParams(vmem_limit_bytes=LATE),
        cost_estimate=COST,
        name="columns_first",
    )(j, d, down, g, *pieces)


def columns_next(u, down, g, narrow):
    parts, two, rows, share = u.shape
    lat = down.shape[3]
    return pl.pallas_call(
        columns_next_kernel,
        out_shape=shape(parts * rows, share),
        in_specs=[VMEM] * 4,
        out_specs=VMEM,
        compiler_params=pltpu.CompilerParams(vmem_limit_bytes=LATE),
        cost_estimate=COST,
        name="columns_next",
    )(u, down, g, narrow)


def first_terms_kernel(d_ref, u_ref, first_ref, out_ref):
    parts, three, rows, share = d_ref.shape
    lat = out_ref.shape[2]
    total = parts * rows
    for at, start in ((0, 0), (1, lat + LANES)):
        down = first_ref[:, :rows, start : start + lat].reshape(total, lat)
        up = first_ref[:, rows:, start : start + lat].reshape(total, lat)
        out_ref[at] = rows_dot(d_ref[:, at].reshape(total, share), down) + rows_dot(u_ref[:, at].reshape(total, share), up)


def first_terms(d, u, first, lat):
    share = d.shape[3]
    return pl.pallas_call(
        first_terms_kernel,
        out_shape=shape(2, share, lat, dtype=F32),
        in_specs=[VMEM] * 3,
        out_specs=VMEM,
        compiler_params=pltpu.CompilerParams(vmem_limit_bytes=LATE),
        cost_estimate=COST,
        name="first_terms",
    )(d, u, first)


def terms_kernel(j_ref, d_ref, x1_ref, y1d_ref, y1u_ref, part_ref, g_ref, *rest):
    pieces, out_ref, second_ref = rest[:-2], rest[-2], rest[-1]
    parts, three, rows, share = d_ref.shape
    lat = second_ref.shape[2] // 2
    total = parts * rows
    restore(j_ref[0], pieces, second_ref)

    def half(i, start):
        return second_ref[:, i * rows : (i + 1) * rows, start : start + lat].reshape(total, lat)

    first = part_ref[0] + rows_dot(d_ref[:, 2].reshape(total, share), half(0, 0))
    first += rows_dot(x1_ref[:, 0].reshape(total, share), half(1, 0))
    out_ref[0, 0] = (first * g_ref[...].astype(F32)).astype(BF16)
    second = part_ref[1] + rows_dot(y1d_ref[...], half(0, lat))
    second += rows_dot(y1u_ref[...], half(1, lat))
    out_ref[0, 1] = second.astype(BF16)


def terms(j, d, x1, y1d, y1u, part, g, pieces):
    parts, three, rows, share = d.shape
    narrow = pieces[0].shape
    return pl.pallas_call(
        terms_kernel,
        out_shape=shape(1, 2, share, narrow[1] // 2),
        in_specs=[SMEM] + [VMEM] * (6 + len(pieces)),
        out_specs=VMEM,
        scratch_shapes=[pltpu.VMEM((parts,) + narrow, BF16)],
        compiler_params=pltpu.CompilerParams(vmem_limit_bytes=LATE),
        cost_estimate=COST,
        name="terms",
    )(j, d, x1, y1d, y1u, part, g, *pieces)


def per_device(weights, gain_model, gain_latent, saved_down, saved_up, grad_start):
    ranks = lax.axis_size("pipe")
    replicas = lax.axis_size("dp")
    j = lax.axis_index("dp")
    share = weights.shape[2] // replicas
    own_down = lax.dynamic_slice(weights, (0, 0, j * share, 0), (1, 1, share, weights.shape[3]))
    own_g = lax.dynamic_slice_in_dim(gain_model, j * share, share, 1)

    def mirror(block):
        return lax.ppermute(block, "pipe", [(i, ranks - 1 - i) for i in range(ranks)])

    def to_before(block):
        return lax.ppermute(block, "pipe", [(i + 1, i) for i in range(ranks - 1)])

    def exchange(blocks):
        return lax.all_to_all(blocks, "dp", 0, 0, tiled=True)

    packed, x0u, y0u, x1u = prepare(saved_down, saved_up, grad_start, replicas)
    packed, x0u, y0u, x1u, saved_down, grad_start = lax.optimization_barrier((packed, x0u, y0u, x1u, saved_down, grad_start))
    x0u, y0u, x1u = mirror(x0u), mirror(y0u), mirror(x1u)
    d_s = exchange(packed)
    z0d, before, k1d, c1d, ab1d = first_step(saved_down, grad_start, weights, gain_model, gain_latent)
    y1d = to_before(z0d)
    column_g = own_g.reshape(share, 1)
    x0u, before, own_down, own_g, column_g = lax.optimization_barrier((x0u, before, own_down, own_g, column_g))
    k0u, c0u, ab0u = latent_side(x0u, weights, gain_model, gain_latent)
    narrow = narrow_step(y0u, weights, gain_latent, k0u, c0u, ab0u, before)
    narrow, y1d = lax.optimization_barrier((narrow, y1d))
    first_pieces = gather_pieces(narrow, "dp")
    far = len(first_pieces) - 1
    z0u, u_packed = input_step(x0u, y0u, weights, gain_model, narrow, replicas)
    y1u = to_before(z0u)
    u_packed, x1u, d_s, *first_pieces[1:far] = lax.optimization_barrier((u_packed, x1u, d_s, *first_pieces[1:far]))
    u_s = exchange(u_packed)
    second, x1_packed = second_step(x1u, y1d, y1u, weights, gain_model, gain_latent, c1d, ab1d, k1d, replicas)
    second_pieces = gather_pieces(second, "dp")
    z0d_s, first = columns_first(j[None], d_s, own_down, own_g, first_pieces)
    y1d_s = to_before(z0d_s)
    u_s, first, x1_packed, *second_pieces[1:far] = lax.optimization_barrier((u_s, first, x1_packed, *second_pieces[1:far]))
    x1_s = exchange(x1_packed)
    z0u_s = columns_next(u_s, own_down, own_g, first)
    y1u_s = to_before(z0u_s)
    part = first_terms(d_s, u_s, first, gain_latent.shape[1])
    return terms(j[None], d_s, x1_s, y1d_s, y1u_s, part, column_g, second_pieces)


def solution(mesh):
    placed = (
        P("pipe", None, None, None),
        P("pipe", None),
        P("pipe", None),
        P("pipe", None, "dp", None),
        P("pipe", None, "dp", None),
        P(None, "pipe", "dp", None),
    )
    return jax.shard_map(
        per_device,
        mesh=mesh,
        in_specs=placed,
        out_specs=P("pipe", None, "dp", None),
        check_vma=False,
    )
```

```python
import functools

import jax
import jax.numpy as jnp
from jax import lax
from jax.experimental import pallas as pl
from jax.experimental.pallas import tpu as pltpu
from jax.sharding import PartitionSpec as P

EPS = 1e-06
LANES = 128
ANY = pl.BlockSpec(memory_space=pl.ANY)
VMEM = pl.BlockSpec(memory_space=pltpu.VMEM)
SMEM = pl.BlockSpec(memory_space=pltpu.SMEM)
LIMIT = 62 * 1024 * 1024
LATE = 32 * 1024 * 1024
COST = pl.CostEstimate(flops=1, bytes_accessed=1, transcendentals=0)
F32 = jnp.float32
BF16 = jnp.bfloat16


def rows_dot(left, right):
    return lax.dot_general(left, right, (((0,), (0,)), ((), ())), preferred_element_type=F32)


def dot_t(left, right):
    return lax.dot_general(left, right, (((1,), (1,)), ((), ())), preferred_element_type=F32)


def dot(left, right):
    return jnp.dot(left, right, preferred_element_type=F32)


def norm_scale(v):
    return lax.rsqrt(jnp.mean(v * v, axis=-1, keepdims=True) + EPS)


def with_scalar(aq, s):
    high = s.astype(BF16).astype(F32)
    at = lax.broadcasted_iota(jnp.int32, (aq.shape[0], LANES), 1)
    tail = jnp.where(at == 0, high, jnp.where(at == 1, s - high, 0.0)).astype(BF16)
    return jnp.concatenate([aq, tail], 1)


def pack_into(out, sources):
    parts, share = out.shape[0], out.shape[3]
    for i, source in enumerate(sources):
        for d in range(parts):
            out[d, i] = source[:, d * share : (d + 1) * share]


def pack_kernel(*refs):
    pack_into(refs[-1], refs[:-1])


def pack(blocks, parts):
    rows, width = blocks[0].shape
    count = len(blocks)
    return pl.pallas_call(
        pack_kernel,
        out_shape=shape(parts, count, rows, width // parts),
        in_specs=[VMEM] * count,
        out_specs=VMEM,
        compiler_params=pltpu.CompilerParams(vmem_limit_bytes=LIMIT),
        cost_estimate=COST,
        name="pack",
    )(*blocks)


def run_copies(pairs, sems):
    copies = [pltpu.make_async_copy(source, target, sems.at[i]) for i, (source, target) in enumerate(pairs)]
    for copy in copies:
        copy.start()
    for copy in copies:
        copy.wait()


def prepare_kernel(down_ref, up_ref, start_ref, packed_ref, x0_ref, y0_ref, x1_ref, sems):
    parts, three, rows, share = packed_ref.shape
    pairs = []
    for i, source in enumerate((down_ref.at[0, 0], start_ref.at[0, 0], down_ref.at[0, 1])):
        for d in range(parts):
            pairs.append((source.at[:, pl.ds(d * share, share)], packed_ref.at[d, i]))
    pairs += [(up_ref.at[0, 0], x0_ref), (start_ref.at[1, 0], y0_ref), (up_ref.at[0, 1], x1_ref)]
    run_copies(pairs, sems)


def prepare(saved_down, saved_up, grad_start, parts):
    rows, width = saved_down.shape[2:]
    share = width // parts
    if share % LANES:
        x0, y0, x1 = saved_up[0, 0], grad_start[1, 0], saved_up[0, 1]
        return pack([saved_down[0, 0], grad_start[0, 0], saved_down[0, 1]], parts), x0, y0, x1
    return pl.pallas_call(
        prepare_kernel,
        out_shape=[shape(parts, 3, rows, share)] + [shape(rows, width)] * 3,
        in_specs=[ANY] * 3,
        out_specs=[VMEM] * 4,
        scratch_shapes=[pltpu.SemaphoreType.DMA((3 * parts + 3,))],
        compiler_params=pltpu.CompilerParams(vmem_limit_bytes=LIMIT),
        cost_estimate=COST,
        name="prepare",
    )(saved_down, saved_up, grad_start)


def shape(*dims, dtype=BF16):
    return jax.ShapeDtypeStruct(dims, dtype)


CHUNKS = 4


def load_chunks(source, buffer, sems):
    chunk = buffer.shape[0] // CHUNKS
    copies = []
    for i in range(CHUNKS):
        part = pl.ds(i * chunk, chunk)
        copies.append(pltpu.make_async_copy(source.at[part], buffer.at[part], sems.at[i]))
    for copy in copies:
        copy.start()
    return copies


def chunked_dot(left, copies, buffer):
    chunk = buffer.shape[0] // CHUNKS
    total = None
    for i, copy in enumerate(copies):
        copy.wait()
        part = dot(left[:, i * chunk : (i + 1) * chunk], buffer[i * chunk : (i + 1) * chunk, :])
        total = part if total is None else total + part
    return total


def latent_gradient(u, c, a, b):
    q = b * (u - c * b * b * jnp.mean(u * c, axis=-1, keepdims=True))
    return (q * a).astype(BF16)


def next_latent(c, a, h, k_ref, c_ref, ab_ref):
    b = norm_scale(c)
    k_ref[...] = (c * b * h).astype(BF16)
    c_ref[...] = c
    at = lax.broadcasted_iota(jnp.int32, (c.shape[0], LANES), 1)
    ab_ref[...] = jnp.where(at == 0, a, b)


def first_kernel(stacked, x_ref, y_ref, w_ref, g_ref, h_ref, *rest):
    rest, (down, up, sem0, sem1) = rest[:-4], rest[-4:]
    copies0 = load_chunks(w_ref.at[0, 0], down, sem0)
    copies1 = load_chunks(w_ref.at[0, 1], up, sem1)
    if stacked:
        x_ref, x1_ref, y_ref = x_ref.at[0, 0], x_ref.at[0, 1], y_ref.at[0, 0]
        z_ref, narrow_ref, k1_ref, c1_ref, ab1_ref = rest
        mine = slice(0, x_ref.shape[0])
    else:
        before_ref, z_ref, narrow_ref = rest
        narrow_ref[: x_ref.shape[0]] = before_ref[...]
        mine = slice(x_ref.shape[0], 2 * x_ref.shape[0])
    rows, width = x_ref.shape
    lat = h_ref.shape[1]
    chunk = width // CHUNKS
    g = g_ref[...].astype(F32)
    h = h_ref[...].astype(F32)
    x = x_ref[...].astype(F32)
    a = norm_scale(x)
    normed = (x * a * g).astype(BF16)
    if stacked:
        x1 = x1_ref[...].astype(F32)
        a1 = norm_scale(x1)
        normed = jnp.concatenate([normed, (x1 * a1 * g).astype(BF16)], 0)
    c = chunked_dot(normed, copies0, down)
    u = chunked_dot(y_ref[...], copies1, up) * h
    if stacked:
        c1 = c[rows:]
        c = c[:rows]
        next_latent(c1, a1, h, k1_ref, c1_ref, ab1_ref)
    b = norm_scale(c)
    narrow_ref[mine, lat + LANES :] = (c * b * h).astype(BF16)
    aq = latent_gradient(u, c, a, b)
    s = a * jnp.sum(aq.astype(F32) * c, axis=-1, keepdims=True) / width
    narrow_ref[mine, : lat + LANES] = with_scalar(aq, s)
    for i in range(CHUNKS):
        cols = slice(i * chunk, (i + 1) * chunk)
        m = dot_t(aq, down[cols, :])
        z = y_ref[:, cols].astype(F32) + m * g[:, cols] - x_ref[:, cols].astype(F32) * s
        z_ref[:, cols] = z.astype(BF16)


def first_step(x, y, weights, g, h, before=None):
    rows, width = x.shape[-2:]
    lat = h.shape[1]
    operands = [x, y, weights, g, h]
    outs = [shape(rows, width)]
    if before is None:
        outs += [shape(rows, 2 * lat + LANES), shape(rows, lat), shape(rows, lat, dtype=F32), shape(rows, LANES, dtype=F32)]
    else:
        outs += [shape(2 * rows, 2 * lat + LANES)]
        operands += [before]
    return pl.pallas_call(
        functools.partial(first_kernel, before is None),
        out_shape=outs,
        in_specs=[VMEM] * 2 + [ANY] + [VMEM] * (len(operands) - 3),
        out_specs=[VMEM] * len(outs),
        scratch_shapes=[pltpu.VMEM((width, lat), BF16)] * 2 + [pltpu.SemaphoreType.DMA((CHUNKS,))] * 2,
        compiler_params=pltpu.CompilerParams(vmem_limit_bytes=LIMIT),
        cost_estimate=COST,
        name="first_step",
    )(*operands)


def latent_kernel(x_ref, w_ref, g_ref, h_ref, k_ref, c_ref, ab_ref, down, sem):
    copies = load_chunks(w_ref.at[0, 0], down, sem)
    x = x_ref[...].astype(F32)
    a = norm_scale(x)
    c = chunked_dot((x * a * g_ref[...].astype(F32)).astype(BF16), copies, down)
    next_latent(c, a, h_ref[...].astype(F32), k_ref, c_ref, ab_ref)


def latent_side(x, weights, g, h):
    rows, width = x.shape
    lat = h.shape[1]
    outs = [shape(rows, lat), shape(rows, lat, dtype=F32), shape(rows, LANES, dtype=F32)]
    return pl.pallas_call(
        latent_kernel,
        out_shape=outs,
        in_specs=[VMEM, ANY, VMEM, VMEM],
        out_specs=[VMEM] * 3,
        scratch_shapes=[pltpu.VMEM((width, lat), BF16), pltpu.SemaphoreType.DMA((CHUNKS,))],
        compiler_params=pltpu.CompilerParams(vmem_limit_bytes=LIMIT),
        cost_estimate=COST,
        name="latent_side",
    )(x, weights, g, h)


def narrow_kernel(y_ref, w_ref, h_ref, k_ref, c_ref, ab_ref, before_ref, narrow_ref, up, sem):
    copies = load_chunks(w_ref.at[0, 1], up, sem)
    rows, width = y_ref.shape
    lat = h_ref.shape[1]
    c, a, b = c_ref[...], ab_ref[:, 0:1], ab_ref[:, 1:2]
    narrow_ref[:rows] = before_ref[...]
    narrow_ref[rows:, lat + LANES :] = k_ref[...]
    aq = latent_gradient(chunked_dot(y_ref[...], copies, up) * h_ref[...].astype(F32), c, a, b)
    s = a * jnp.sum(aq.astype(F32) * c, axis=-1, keepdims=True) / width
    narrow_ref[rows:, : lat + LANES] = with_scalar(aq, s)


def narrow_step(y, weights, h, k, c, ab, before):
    rows, width = y.shape
    lat = h.shape[1]
    return pl.pallas_call(
        narrow_kernel,
        out_shape=shape(2 * rows, 2 * lat + LANES),
        in_specs=[VMEM, ANY] + [VMEM] * 5,
        out_specs=VMEM,
        scratch_shapes=[pltpu.VMEM((width, lat), BF16), pltpu.SemaphoreType.DMA((CHUNKS,))],
        compiler_params=pltpu.CompilerParams(vmem_limit_bytes=LIMIT),
        cost_estimate=COST,
        name="narrow_step",
    )(y, weights, h, k, c, ab, before)


def input_kernel(x_ref, y_ref, w_ref, g_ref, narrow_ref, z_ref, packed_ref, down, sem):
    copies = load_chunks(w_ref.at[0, 0], down, sem)
    rows, width = x_ref.shape
    lat = down.shape[1]
    chunk = width // CHUNKS
    pack_into(packed_ref, [x_ref, y_ref])
    aq = narrow_ref[rows:, :lat]
    s = narrow_ref[rows:, lat : lat + 1].astype(F32) + narrow_ref[rows:, lat + 1 : lat + 2].astype(F32)
    for i, copy in enumerate(copies):
        copy.wait()
        cols = slice(i * chunk, (i + 1) * chunk)
        m = dot_t(aq, down[cols, :])
        z = y_ref[:, cols].astype(F32) + m * g_ref[:, cols].astype(F32) - x_ref[:, cols].astype(F32) * s
        z_ref[:, cols] = z.astype(BF16)


def input_step(x, y, weights, g, narrow, parts):
    rows, width = x.shape
    lat = weights.shape[3]
    return pl.pallas_call(
        input_kernel,
        out_shape=[shape(rows, width), shape(parts, 2, rows, width // parts)],
        in_specs=[VMEM] * 2 + [ANY] + [VMEM] * 2,
        out_specs=[VMEM] * 2,
        scratch_shapes=[pltpu.VMEM((width, lat), BF16), pltpu.SemaphoreType.DMA((CHUNKS,))],
        compiler_params=pltpu.CompilerParams(vmem_limit_bytes=LIMIT),
        cost_estimate=COST,
        name="input_step",
    )(x, y, weights, g, narrow)


def second_kernel(x_ref, y0_ref, y1_ref, w_ref, g_ref, h_ref, c0_ref, ab0_ref, k0_ref, out_ref, packed_ref, down, up, sem0, sem1):
    copies0 = load_chunks(w_ref.at[0, 0], down, sem0)
    copies1 = load_chunks(w_ref.at[0, 1], up, sem1)
    rows, width = x_ref.shape
    lat = h_ref.shape[1]
    pack_into(packed_ref, [x_ref])
    h = h_ref[...].astype(F32)
    x = x_ref[...].astype(F32)
    a = norm_scale(x)
    c = chunked_dot((x * a * g_ref[...].astype(F32)).astype(BF16), copies0, down)
    b = norm_scale(c)
    out_ref[:rows, lat:] = k0_ref[...]
    out_ref[rows:, lat:] = (c * b * h).astype(BF16)
    u = chunked_dot(jnp.concatenate([y0_ref[...], y1_ref[...]], 0), copies1, up) * h
    out_ref[:rows, :lat] = latent_gradient(u[:rows], c0_ref[...], ab0_ref[:, 0:1], ab0_ref[:, 1:2])
    out_ref[rows:, :lat] = latent_gradient(u[rows:], c, a, b)


def second_step(x, y0, y1, weights, g, h, c0, ab0, k0, parts):
    rows, width = x.shape
    lat = h.shape[1]
    return pl.pallas_call(
        second_kernel,
        out_shape=[shape(2 * rows, 2 * lat), shape(parts, 1, rows, width // parts)],
        in_specs=[VMEM] * 3 + [ANY] + [VMEM] * 5,
        out_specs=[VMEM] * 2,
        scratch_shapes=[pltpu.VMEM((width, lat), BF16)] * 2 + [pltpu.SemaphoreType.DMA((CHUNKS,))] * 2,
        compiler_params=pltpu.CompilerParams(vmem_limit_bytes=LIMIT),
        cost_estimate=COST,
        name="second_step",
    )(x, y0, y1, weights, g, h, c0, ab0, k0)


def held_order(parts):
    far = list(range(parts - 2, 0, -2))
    return [0] + far + [p ^ 1 for p in [0] + far]


def gather_pieces(block, axis):
    parts = lax.axis_size(axis)

    def across(held, apart):
        return lax.ppermute(held, axis, [(i, i ^ apart) for i in range(parts)])

    pieces = [block] + [across(block, apart) for apart in range(parts - 2, 0, -2)]
    return pieces + [across(jnp.concatenate(pieces, 0), 1)]


def restore(j, pieces, out):
    parts, rows = out.shape[:2]
    order, at = held_order(parts), 0
    for piece in pieces:
        for i in range(piece.shape[0] // rows):
            out[j ^ order[at]] = piece[i * rows : (i + 1) * rows, :]
            at += 1


def columns_of(x, y, narrow, down, g):
    parts, rows, share = x.shape
    lat = down.shape[3]
    narrow = narrow.reshape(parts * rows, narrow.shape[2])
    s = narrow[:, lat : lat + 1].astype(F32) + narrow[:, lat + 1 : lat + 2].astype(F32)
    m = dot_t(narrow[:, :lat], down[0, 0])
    x = x.reshape(parts * rows, share).astype(F32)
    y = y.reshape(parts * rows, share).astype(F32)
    return (y + m * g[...].astype(F32) - x * s).astype(BF16)


def columns_first_kernel(j_ref, d_ref, down_ref, g_ref, *rest):
    pieces, z_ref, narrow_ref = rest[:-2], rest[-2], rest[-1]
    restore(j_ref[0], pieces, narrow_ref)
    rows = d_ref.shape[2]
    z_ref[...] = columns_of(d_ref[:, 0], d_ref[:, 1], narrow_ref[:, :rows, :], down_ref, g_ref)


def columns_next_kernel(u_ref, down_ref, g_ref, narrow_ref, z_ref):
    rows = u_ref.shape[2]
    z_ref[...] = columns_of(u_ref[:, 0], u_ref[:, 1], narrow_ref[:, rows:, :], down_ref, g_ref)


def columns_first(j, d, down, g, pieces):
    parts, two, rows, share = d.shape
    lat = down.shape[3]
    return pl.pallas_call(
        columns_first_kernel,
        out_shape=[shape(parts * rows, share), shape(parts, *pieces[0].shape)],
        in_specs=[SMEM] + [VMEM] * (3 + len(pieces)),
        out_specs=[VMEM, VMEM],
        compiler_params=pltpu.CompilerParams(vmem_limit_bytes=LATE),
        cost_estimate=COST,
        name="columns_first",
    )(j, d, down, g, *pieces)


def columns_next(u, down, g, narrow):
    parts, two, rows, share = u.shape
    lat = down.shape[3]
    return pl.pallas_call(
        columns_next_kernel,
        out_shape=shape(parts * rows, share),
        in_specs=[VMEM] * 4,
        out_specs=VMEM,
        compiler_params=pltpu.CompilerParams(vmem_limit_bytes=LATE),
        cost_estimate=COST,
        name="columns_next",
    )(u, down, g, narrow)


def first_terms_kernel(d_ref, u_ref, first_ref, out_ref):
    parts, three, rows, share = d_ref.shape
    lat = out_ref.shape[2]
    total = parts * rows
    for at, start in ((0, 0), (1, lat + LANES)):
        down = first_ref[:, :rows, start : start + lat].reshape(total, lat)
        up = first_ref[:, rows:, start : start + lat].reshape(total, lat)
        out_ref[at] = rows_dot(d_ref[:, at].reshape(total, share), down) + rows_dot(u_ref[:, at].reshape(total, share), up)


def first_terms(d, u, first, lat):
    share = d.shape[3]
    return pl.pallas_call(
        first_terms_kernel,
        out_shape=shape(2, share, lat, dtype=F32),
        in_specs=[VMEM] * 3,
        out_specs=VMEM,
        compiler_params=pltpu.CompilerParams(vmem_limit_bytes=LATE),
        cost_estimate=COST,
        name="first_terms",
    )(d, u, first)


def terms_kernel(j_ref, d_ref, x1_ref, y1d_ref, y1u_ref, part_ref, g_ref, *rest):
    pieces, out_ref, second_ref = rest[:-2], rest[-2], rest[-1]
    parts, three, rows, share = d_ref.shape
    lat = second_ref.shape[2] // 2
    total = parts * rows
    restore(j_ref[0], pieces, second_ref)

    def half(i, start):
        return second_ref[:, i * rows : (i + 1) * rows, start : start + lat].reshape(total, lat)

    first = part_ref[0] + rows_dot(d_ref[:, 2].reshape(total, share), half(0, 0))
    first += rows_dot(x1_ref[:, 0].reshape(total, share), half(1, 0))
    out_ref[0, 0] = (first * g_ref[...].astype(F32)).astype(BF16)
    second = part_ref[1] + rows_dot(y1d_ref[...], half(0, lat))
    second += rows_dot(y1u_ref[...], half(1, lat))
    out_ref[0, 1] = second.astype(BF16)


def terms(j, d, x1, y1d, y1u, part, g, pieces):
    parts, three, rows, share = d.shape
    narrow = pieces[0].shape
    return pl.pallas_call(
        terms_kernel,
        out_shape=shape(1, 2, share, narrow[1] // 2),
        in_specs=[SMEM] + [VMEM] * (6 + len(pieces)),
        out_specs=VMEM,
        scratch_shapes=[pltpu.VMEM((parts,) + narrow, BF16)],
        compiler_params=pltpu.CompilerParams(vmem_limit_bytes=LATE),
        cost_estimate=COST,
        name="terms",
    )(j, d, x1, y1d, y1u, part, g, *pieces)


def per_device(weights, gain_model, gain_latent, saved_down, saved_up, grad_start):
    ranks = lax.axis_size("pipe")
    replicas = lax.axis_size("dp")
    j = lax.axis_index("dp")
    share = weights.shape[2] // replicas
    own_down = lax.dynamic_slice(weights, (0, 0, j * share, 0), (1, 1, share, weights.shape[3]))
    own_g = lax.dynamic_slice_in_dim(gain_model, j * share, share, 1)

    def mirror(block):
        return lax.ppermute(block, "pipe", [(i, ranks - 1 - i) for i in range(ranks)])

    def to_before(block):
        return lax.ppermute(block, "pipe", [(i + 1, i) for i in range(ranks - 1)])

    def exchange(blocks):
        return lax.all_to_all(blocks, "dp", 0, 0, tiled=True)

    packed, x0u, y0u, x1u = prepare(saved_down, saved_up, grad_start, replicas)
    packed, x0u, y0u, x1u, saved_down, grad_start = lax.optimization_barrier((packed, x0u, y0u, x1u, saved_down, grad_start))
    x0u, y0u, x1u = mirror(x0u), mirror(y0u), mirror(x1u)
    d_s = exchange(packed)
    z0d, before, k1d, c1d, ab1d = first_step(saved_down, grad_start, weights, gain_model, gain_latent)
    y1d = to_before(z0d)
    column_g = own_g.reshape(share, 1)
    x0u, before, own_down, own_g, column_g = lax.optimization_barrier((x0u, before, own_down, own_g, column_g))
    k0u, c0u, ab0u = latent_side(x0u, weights, gain_model, gain_latent)
    narrow = narrow_step(y0u, weights, gain_latent, k0u, c0u, ab0u, before)
    first_pieces = gather_pieces(narrow, "dp")
    far = len(first_pieces) - 1
    z0u, u_packed = input_step(x0u, y0u, weights, gain_model, narrow, replicas)
    y1u = to_before(z0u)
    u_packed, x1u, y1d, d_s, *first_pieces[1:far] = lax.optimization_barrier((u_packed, x1u, y1d, d_s, *first_pieces[1:far]))
    u_s = exchange(u_packed)
    second, x1_packed = second_step(x1u, y1d, y1u, weights, gain_model, gain_latent, c1d, ab1d, k1d, replicas)
    second_pieces = gather_pieces(second, "dp")
    z0d_s, first = columns_first(j[None], d_s, own_down, own_g, first_pieces)
    y1d_s = to_before(z0d_s)
    z0u_s = columns_next(u_s, own_down, own_g, first)
    z0u_s, x1_packed, *second_pieces[1:far] = lax.optimization_barrier((z0u_s, x1_packed, *second_pieces[1:far]))
    x1_s = exchange(x1_packed)
    y1u_s = to_before(z0u_s)
    part = first_terms(d_s, u_s, first, gain_latent.shape[1])
    return terms(j[None], d_s, x1_s, y1d_s, y1u_s, part, column_g, second_pieces)


def solution(mesh):
    placed = (
        P("pipe", None, None, None),
        P("pipe", None),
        P("pipe", None),
        P("pipe", None, "dp", None),
        P("pipe", None, "dp", None),
        P(None, "pipe", "dp", None),
    )
    return jax.shard_map(
        per_device,
        mesh=mesh,
        in_specs=placed,
        out_specs=P("pipe", None, "dp", None),
        check_vma=False,
    )
```

```python
import functools

import jax
import jax.numpy as jnp
from jax import lax
from jax.experimental import pallas as pl
from jax.experimental.pallas import tpu as pltpu
from jax.sharding import PartitionSpec as P

EPS = 1e-06
LANES = 128
ANY = pl.BlockSpec(memory_space=pl.ANY)
VMEM = pl.BlockSpec(memory_space=pltpu.VMEM)
SMEM = pl.BlockSpec(memory_space=pltpu.SMEM)
LIMIT = 62 * 1024 * 1024
LATE = 32 * 1024 * 1024
COST = pl.CostEstimate(flops=1, bytes_accessed=1, transcendentals=0)
F32 = jnp.float32
BF16 = jnp.bfloat16


def rows_dot(left, right):
    return lax.dot_general(left, right, (((0,), (0,)), ((), ())), preferred_element_type=F32)


def dot_t(left, right):
    return lax.dot_general(left, right, (((1,), (1,)), ((), ())), preferred_element_type=F32)


def dot(left, right):
    return jnp.dot(left, right, preferred_element_type=F32)


def norm_scale(v):
    return lax.rsqrt(jnp.mean(v * v, axis=-1, keepdims=True) + EPS)


def with_scalar(aq, s):
    high = s.astype(BF16).astype(F32)
    at = lax.broadcasted_iota(jnp.int32, (aq.shape[0], LANES), 1)
    tail = jnp.where(at == 0, high, jnp.where(at == 1, s - high, 0.0)).astype(BF16)
    return jnp.concatenate([aq, tail], 1)


def pack_into(out, sources):
    parts, share = out.shape[0], out.shape[3]
    for i, source in enumerate(sources):
        for d in range(parts):
            out[d, i] = source[:, d * share : (d + 1) * share]


def pack_kernel(*refs):
    pack_into(refs[-1], refs[:-1])


def pack(blocks, parts):
    rows, width = blocks[0].shape
    count = len(blocks)
    return pl.pallas_call(
        pack_kernel,
        out_shape=shape(parts, count, rows, width // parts),
        in_specs=[VMEM] * count,
        out_specs=VMEM,
        compiler_params=pltpu.CompilerParams(vmem_limit_bytes=LIMIT),
        cost_estimate=COST,
        name="pack",
    )(*blocks)


def run_copies(pairs, sems):
    copies = [pltpu.make_async_copy(source, target, sems.at[i]) for i, (source, target) in enumerate(pairs)]
    for copy in copies:
        copy.start()
    for copy in copies:
        copy.wait()


def prepare_kernel(down_ref, up_ref, start_ref, packed_ref, x0_ref, y0_ref, x1_ref, sems):
    parts, three, rows, share = packed_ref.shape
    pairs = []
    for i, source in enumerate((down_ref.at[0, 0], start_ref.at[0, 0], down_ref.at[0, 1])):
        for d in range(parts):
            pairs.append((source.at[:, pl.ds(d * share, share)], packed_ref.at[d, i]))
    pairs += [(up_ref.at[0, 0], x0_ref), (start_ref.at[1, 0], y0_ref), (up_ref.at[0, 1], x1_ref)]
    run_copies(pairs, sems)


def prepare(saved_down, saved_up, grad_start, parts):
    rows, width = saved_down.shape[2:]
    share = width // parts
    if share % LANES:
        x0, y0, x1 = saved_up[0, 0], grad_start[1, 0], saved_up[0, 1]
        return pack([saved_down[0, 0], grad_start[0, 0], saved_down[0, 1]], parts), x0, y0, x1
    return pl.pallas_call(
        prepare_kernel,
        out_shape=[shape(parts, 3, rows, share)] + [shape(rows, width)] * 3,
        in_specs=[ANY] * 3,
        out_specs=[VMEM] * 4,
        scratch_shapes=[pltpu.SemaphoreType.DMA((3 * parts + 3,))],
        compiler_params=pltpu.CompilerParams(vmem_limit_bytes=LIMIT),
        cost_estimate=COST,
        name="prepare",
    )(saved_down, saved_up, grad_start)


def shape(*dims, dtype=BF16):
    return jax.ShapeDtypeStruct(dims, dtype)


CHUNKS = 4


def load_chunks(source, buffer, sems):
    chunk = buffer.shape[0] // CHUNKS
    copies = []
    for i in range(CHUNKS):
        part = pl.ds(i * chunk, chunk)
        copies.append(pltpu.make_async_copy(source.at[part], buffer.at[part], sems.at[i]))
    for copy in copies:
        copy.start()
    return copies


def chunked_dot(left, copies, buffer):
    chunk = buffer.shape[0] // CHUNKS
    total = None
    for i, copy in enumerate(copies):
        copy.wait()
        part = dot(left[:, i * chunk : (i + 1) * chunk], buffer[i * chunk : (i + 1) * chunk, :])
        total = part if total is None else total + part
    return total


def latent_gradient(u, c, a, b):
    q = b * (u - c * b * b * jnp.mean(u * c, axis=-1, keepdims=True))
    return (q * a).astype(BF16)


def next_latent(c, a, h, k_ref, c_ref, ab_ref):
    b = norm_scale(c)
    k_ref[...] = (c * b * h).astype(BF16)
    c_ref[...] = c
    at = lax.broadcasted_iota(jnp.int32, (c.shape[0], LANES), 1)
    ab_ref[...] = jnp.where(at == 0, a, b)


def first_kernel(stacked, x_ref, y_ref, w_ref, g_ref, h_ref, *rest):
    rest, (down, up, sem0, sem1) = rest[:-4], rest[-4:]
    copies0 = load_chunks(w_ref.at[0, 0], down, sem0)
    copies1 = load_chunks(w_ref.at[0, 1], up, sem1)
    if stacked:
        x_ref, x1_ref, y_ref = x_ref.at[0, 0], x_ref.at[0, 1], y_ref.at[0, 0]
        z_ref, narrow_ref, k1_ref, c1_ref, ab1_ref = rest
        mine = slice(0, x_ref.shape[0])
    else:
        before_ref, z_ref, narrow_ref = rest
        narrow_ref[: x_ref.shape[0]] = before_ref[...]
        mine = slice(x_ref.shape[0], 2 * x_ref.shape[0])
    rows, width = x_ref.shape
    lat = h_ref.shape[1]
    chunk = width // CHUNKS
    g = g_ref[...].astype(F32)
    h = h_ref[...].astype(F32)
    x = x_ref[...].astype(F32)
    a = norm_scale(x)
    normed = (x * a * g).astype(BF16)
    if stacked:
        x1 = x1_ref[...].astype(F32)
        a1 = norm_scale(x1)
        normed = jnp.concatenate([normed, (x1 * a1 * g).astype(BF16)], 0)
    c = chunked_dot(normed, copies0, down)
    u = chunked_dot(y_ref[...], copies1, up) * h
    if stacked:
        c1 = c[rows:]
        c = c[:rows]
        next_latent(c1, a1, h, k1_ref, c1_ref, ab1_ref)
    b = norm_scale(c)
    narrow_ref[mine, lat + LANES :] = (c * b * h).astype(BF16)
    aq = latent_gradient(u, c, a, b)
    s = a * jnp.sum(aq.astype(F32) * c, axis=-1, keepdims=True) / width
    narrow_ref[mine, : lat + LANES] = with_scalar(aq, s)
    for i in range(CHUNKS):
        cols = slice(i * chunk, (i + 1) * chunk)
        m = dot_t(aq, down[cols, :])
        z = y_ref[:, cols].astype(F32) + m * g[:, cols] - x_ref[:, cols].astype(F32) * s
        z_ref[:, cols] = z.astype(BF16)


def first_step(x, y, weights, g, h, before=None):
    rows, width = x.shape[-2:]
    lat = h.shape[1]
    operands = [x, y, weights, g, h]
    outs = [shape(rows, width)]
    if before is None:
        outs += [shape(rows, 2 * lat + LANES), shape(rows, lat), shape(rows, lat, dtype=F32), shape(rows, LANES, dtype=F32)]
    else:
        outs += [shape(2 * rows, 2 * lat + LANES)]
        operands += [before]
    return pl.pallas_call(
        functools.partial(first_kernel, before is None),
        out_shape=outs,
        in_specs=[VMEM] * 2 + [ANY] + [VMEM] * (len(operands) - 3),
        out_specs=[VMEM] * len(outs),
        scratch_shapes=[pltpu.VMEM((width, lat), BF16)] * 2 + [pltpu.SemaphoreType.DMA((CHUNKS,))] * 2,
        compiler_params=pltpu.CompilerParams(vmem_limit_bytes=LIMIT),
        cost_estimate=COST,
        name="first_step",
    )(*operands)


def latent_kernel(x_ref, w_ref, g_ref, h_ref, k_ref, c_ref, ab_ref, down, sem):
    copies = load_chunks(w_ref.at[0, 0], down, sem)
    x = x_ref[...].astype(F32)
    a = norm_scale(x)
    c = chunked_dot((x * a * g_ref[...].astype(F32)).astype(BF16), copies, down)
    next_latent(c, a, h_ref[...].astype(F32), k_ref, c_ref, ab_ref)


def latent_side(x, weights, g, h):
    rows, width = x.shape
    lat = h.shape[1]
    outs = [shape(rows, lat), shape(rows, lat, dtype=F32), shape(rows, LANES, dtype=F32)]
    return pl.pallas_call(
        latent_kernel,
        out_shape=outs,
        in_specs=[VMEM, ANY, VMEM, VMEM],
        out_specs=[VMEM] * 3,
        scratch_shapes=[pltpu.VMEM((width, lat), BF16), pltpu.SemaphoreType.DMA((CHUNKS,))],
        compiler_params=pltpu.CompilerParams(vmem_limit_bytes=LIMIT),
        cost_estimate=COST,
        name="latent_side",
    )(x, weights, g, h)


def narrow_kernel(y_ref, w_ref, h_ref, k_ref, c_ref, ab_ref, before_ref, narrow_ref, up, sem):
    copies = load_chunks(w_ref.at[0, 1], up, sem)
    rows, width = y_ref.shape
    lat = h_ref.shape[1]
    c, a, b = c_ref[...], ab_ref[:, 0:1], ab_ref[:, 1:2]
    narrow_ref[:rows] = before_ref[...]
    narrow_ref[rows:, lat + LANES :] = k_ref[...]
    aq = latent_gradient(chunked_dot(y_ref[...], copies, up) * h_ref[...].astype(F32), c, a, b)
    s = a * jnp.sum(aq.astype(F32) * c, axis=-1, keepdims=True) / width
    narrow_ref[rows:, : lat + LANES] = with_scalar(aq, s)


def narrow_step(y, weights, h, k, c, ab, before):
    rows, width = y.shape
    lat = h.shape[1]
    return pl.pallas_call(
        narrow_kernel,
        out_shape=shape(2 * rows, 2 * lat + LANES),
        in_specs=[VMEM, ANY] + [VMEM] * 5,
        out_specs=VMEM,
        scratch_shapes=[pltpu.VMEM((width, lat), BF16), pltpu.SemaphoreType.DMA((CHUNKS,))],
        compiler_params=pltpu.CompilerParams(vmem_limit_bytes=LIMIT),
        cost_estimate=COST,
        name="narrow_step",
    )(y, weights, h, k, c, ab, before)


def input_kernel(x_ref, y_ref, w_ref, g_ref, narrow_ref, z_ref, packed_ref, down, sem):
    copies = load_chunks(w_ref.at[0, 0], down, sem)
    rows, width = x_ref.shape
    lat = down.shape[1]
    chunk = width // CHUNKS
    pack_into(packed_ref, [x_ref, y_ref])
    aq = narrow_ref[rows:, :lat]
    s = narrow_ref[rows:, lat : lat + 1].astype(F32) + narrow_ref[rows:, lat + 1 : lat + 2].astype(F32)
    for i, copy in enumerate(copies):
        copy.wait()
        cols = slice(i * chunk, (i + 1) * chunk)
        m = dot_t(aq, down[cols, :])
        z = y_ref[:, cols].astype(F32) + m * g_ref[:, cols].astype(F32) - x_ref[:, cols].astype(F32) * s
        z_ref[:, cols] = z.astype(BF16)


def input_step(x, y, weights, g, narrow, parts):
    rows, width = x.shape
    lat = weights.shape[3]
    return pl.pallas_call(
        input_kernel,
        out_shape=[shape(rows, width), shape(parts, 2, rows, width // parts)],
        in_specs=[VMEM] * 2 + [ANY] + [VMEM] * 2,
        out_specs=[VMEM] * 2,
        scratch_shapes=[pltpu.VMEM((width, lat), BF16), pltpu.SemaphoreType.DMA((CHUNKS,))],
        compiler_params=pltpu.CompilerParams(vmem_limit_bytes=LIMIT),
        cost_estimate=COST,
        name="input_step",
    )(x, y, weights, g, narrow)


def second_kernel(x_ref, y0_ref, y1_ref, w_ref, g_ref, h_ref, c0_ref, ab0_ref, k0_ref, out_ref, packed_ref, down, up, sem0, sem1):
    copies0 = load_chunks(w_ref.at[0, 0], down, sem0)
    copies1 = load_chunks(w_ref.at[0, 1], up, sem1)
    rows, width = x_ref.shape
    lat = h_ref.shape[1]
    pack_into(packed_ref, [x_ref])
    h = h_ref[...].astype(F32)
    x = x_ref[...].astype(F32)
    a = norm_scale(x)
    c = chunked_dot((x * a * g_ref[...].astype(F32)).astype(BF16), copies0, down)
    b = norm_scale(c)
    out_ref[:rows, lat:] = k0_ref[...]
    out_ref[rows:, lat:] = (c * b * h).astype(BF16)
    u = chunked_dot(jnp.concatenate([y0_ref[...], y1_ref[...]], 0), copies1, up) * h
    out_ref[:rows, :lat] = latent_gradient(u[:rows], c0_ref[...], ab0_ref[:, 0:1], ab0_ref[:, 1:2])
    out_ref[rows:, :lat] = latent_gradient(u[rows:], c, a, b)


def second_step(x, y0, y1, weights, g, h, c0, ab0, k0, parts):
    rows, width = x.shape
    lat = h.shape[1]
    return pl.pallas_call(
        second_kernel,
        out_shape=[shape(2 * rows, 2 * lat), shape(parts, 1, rows, width // parts)],
        in_specs=[VMEM] * 3 + [ANY] + [VMEM] * 5,
        out_specs=[VMEM] * 2,
        scratch_shapes=[pltpu.VMEM((width, lat), BF16)] * 2 + [pltpu.SemaphoreType.DMA((CHUNKS,))] * 2,
        compiler_params=pltpu.CompilerParams(vmem_limit_bytes=LIMIT),
        cost_estimate=COST,
        name="second_step",
    )(x, y0, y1, weights, g, h, c0, ab0, k0)


def held_order(parts):
    far = list(range(parts - 2, 0, -2))
    return [0] + far + [p ^ 1 for p in [0] + far]


def gather_pieces(block, axis):
    parts = lax.axis_size(axis)

    def across(held, apart):
        return lax.ppermute(held, axis, [(i, i ^ apart) for i in range(parts)])

    pieces = [block] + [across(block, apart) for apart in range(parts - 2, 0, -2)]
    return pieces + [across(jnp.concatenate(pieces, 0), 1)]


def gather_split(block, axis):
    parts = lax.axis_size(axis)

    def across(held, apart):
        return lax.ppermute(held, axis, [(i, i ^ apart) for i in range(parts)])

    far = [across(block, apart) for apart in range(parts - 2, 0, -2)]
    return [block, *far, across(block, 1), across(jnp.concatenate(far, 0), 1)]


def restore(j, pieces, out):
    parts, rows = out.shape[:2]
    order, at = held_order(parts), 0
    for piece in pieces:
        for i in range(piece.shape[0] // rows):
            out[j ^ order[at]] = piece[i * rows : (i + 1) * rows, :]
            at += 1


def columns_of(x, y, narrow, down, g):
    parts, rows, share = x.shape
    lat = down.shape[3]
    narrow = narrow.reshape(parts * rows, narrow.shape[2])
    s = narrow[:, lat : lat + 1].astype(F32) + narrow[:, lat + 1 : lat + 2].astype(F32)
    m = dot_t(narrow[:, :lat], down[0, 0])
    x = x.reshape(parts * rows, share).astype(F32)
    y = y.reshape(parts * rows, share).astype(F32)
    return (y + m * g[...].astype(F32) - x * s).astype(BF16)


def columns_first_kernel(j_ref, d_ref, down_ref, g_ref, *rest):
    pieces, z_ref, narrow_ref = rest[:-2], rest[-2], rest[-1]
    restore(j_ref[0], pieces, narrow_ref)
    rows = d_ref.shape[2]
    z_ref[...] = columns_of(d_ref[:, 0], d_ref[:, 1], narrow_ref[:, :rows, :], down_ref, g_ref)


def columns_next_kernel(u_ref, down_ref, g_ref, narrow_ref, z_ref):
    rows = u_ref.shape[2]
    z_ref[...] = columns_of(u_ref[:, 0], u_ref[:, 1], narrow_ref[:, rows:, :], down_ref, g_ref)


def columns_first(j, d, down, g, pieces):
    parts, two, rows, share = d.shape
    lat = down.shape[3]
    return pl.pallas_call(
        columns_first_kernel,
        out_shape=[shape(parts * rows, share), shape(parts, *pieces[0].shape)],
        in_specs=[SMEM] + [VMEM] * (3 + len(pieces)),
        out_specs=[VMEM, VMEM],
        compiler_params=pltpu.CompilerParams(vmem_limit_bytes=LATE),
        cost_estimate=COST,
        name="columns_first",
    )(j, d, down, g, *pieces)


def columns_next(u, down, g, narrow):
    parts, two, rows, share = u.shape
    lat = down.shape[3]
    return pl.pallas_call(
        columns_next_kernel,
        out_shape=shape(parts * rows, share),
        in_specs=[VMEM] * 4,
        out_specs=VMEM,
        compiler_params=pltpu.CompilerParams(vmem_limit_bytes=LATE),
        cost_estimate=COST,
        name="columns_next",
    )(u, down, g, narrow)


def first_terms_kernel(d_ref, u_ref, first_ref, out_ref):
    parts, three, rows, share = d_ref.shape
    lat = out_ref.shape[2]
    total = parts * rows
    for at, start in ((0, 0), (1, lat + LANES)):
        down = first_ref[:, :rows, start : start + lat].reshape(total, lat)
        up = first_ref[:, rows:, start : start + lat].reshape(total, lat)
        out_ref[at] = rows_dot(d_ref[:, at].reshape(total, share), down) + rows_dot(u_ref[:, at].reshape(total, share), up)


def first_terms(d, u, first, lat):
    share = d.shape[3]
    return pl.pallas_call(
        first_terms_kernel,
        out_shape=shape(2, share, lat, dtype=F32),
        in_specs=[VMEM] * 3,
        out_specs=VMEM,
        compiler_params=pltpu.CompilerParams(vmem_limit_bytes=LATE),
        cost_estimate=COST,
        name="first_terms",
    )(d, u, first)


def terms_kernel(j_ref, d_ref, x1_ref, y1d_ref, y1u_ref, part_ref, g_ref, *rest):
    pieces, out_ref, second_ref = rest[:-2], rest[-2], rest[-1]
    parts, three, rows, share = d_ref.shape
    lat = second_ref.shape[2] // 2
    total = parts * rows
    restore(j_ref[0], pieces, second_ref)

    def half(i, start):
        return second_ref[:, i * rows : (i + 1) * rows, start : start + lat].reshape(total, lat)

    first = part_ref[0] + rows_dot(d_ref[:, 2].reshape(total, share), half(0, 0))
    first += rows_dot(x1_ref[:, 0].reshape(total, share), half(1, 0))
    out_ref[0, 0] = (first * g_ref[...].astype(F32)).astype(BF16)
    second = part_ref[1] + rows_dot(y1d_ref[...], half(0, lat))
    second += rows_dot(y1u_ref[...], half(1, lat))
    out_ref[0, 1] = second.astype(BF16)


def terms(j, d, x1, y1d, y1u, part, g, pieces):
    parts, three, rows, share = d.shape
    narrow = pieces[0].shape
    return pl.pallas_call(
        terms_kernel,
        out_shape=shape(1, 2, share, narrow[1] // 2),
        in_specs=[SMEM] + [VMEM] * (6 + len(pieces)),
        out_specs=VMEM,
        scratch_shapes=[pltpu.VMEM((parts,) + narrow, BF16)],
        compiler_params=pltpu.CompilerParams(vmem_limit_bytes=LATE),
        cost_estimate=COST,
        name="terms",
    )(j, d, x1, y1d, y1u, part, g, *pieces)


def per_device(weights, gain_model, gain_latent, saved_down, saved_up, grad_start):
    ranks = lax.axis_size("pipe")
    replicas = lax.axis_size("dp")
    j = lax.axis_index("dp")
    share = weights.shape[2] // replicas
    own_down = lax.dynamic_slice(weights, (0, 0, j * share, 0), (1, 1, share, weights.shape[3]))
    own_g = lax.dynamic_slice_in_dim(gain_model, j * share, share, 1)

    def mirror(block):
        return lax.ppermute(block, "pipe", [(i, ranks - 1 - i) for i in range(ranks)])

    def to_before(block):
        return lax.ppermute(block, "pipe", [(i + 1, i) for i in range(ranks - 1)])

    def exchange(blocks):
        return lax.all_to_all(blocks, "dp", 0, 0, tiled=True)

    packed, x0u, y0u, x1u = prepare(saved_down, saved_up, grad_start, replicas)
    packed, x0u, y0u, x1u, saved_down, grad_start = lax.optimization_barrier((packed, x0u, y0u, x1u, saved_down, grad_start))
    x0u, y0u, x1u = mirror(x0u), mirror(y0u), mirror(x1u)
    d_s = exchange(packed)
    z0d, before, k1d, c1d, ab1d = first_step(saved_down, grad_start, weights, gain_model, gain_latent)
    y1d = to_before(z0d)
    column_g = own_g.reshape(share, 1)
    x0u, before, own_down, own_g, column_g = lax.optimization_barrier((x0u, before, own_down, own_g, column_g))
    k0u, c0u, ab0u = latent_side(x0u, weights, gain_model, gain_latent)
    narrow = narrow_step(y0u, weights, gain_latent, k0u, c0u, ab0u, before)
    first_pieces = gather_pieces(narrow, "dp")
    far = len(first_pieces) - 1
    z0u, u_packed = input_step(x0u, y0u, weights, gain_model, narrow, replicas)
    y1u = to_before(z0u)
    u_packed, x1u, y1d, d_s, *first_pieces[1:far] = lax.optimization_barrier((u_packed, x1u, y1d, d_s, *first_pieces[1:far]))
    u_s = exchange(u_packed)
    second, x1_packed = second_step(x1u, y1d, y1u, weights, gain_model, gain_latent, c1d, ab1d, k1d, replicas)
    second_pieces = gather_split(second, "dp")
    z0d_s, first = columns_first(j[None], d_s, own_down, own_g, first_pieces)
    y1d_s = to_before(z0d_s)
    z0u_s = columns_next(u_s, own_down, own_g, first)
    z0u_s, x1_packed, *second_pieces[1 : far + 1] = lax.optimization_barrier((z0u_s, x1_packed, *second_pieces[1 : far + 1]))
    x1_s = exchange(x1_packed)
    y1u_s = to_before(z0u_s)
    part = first_terms(d_s, u_s, first, gain_latent.shape[1])
    return terms(j[None], d_s, x1_s, y1d_s, y1u_s, part, column_g, second_pieces)


def solution(mesh):
    placed = (
        P("pipe", None, None, None),
        P("pipe", None),
        P("pipe", None),
        P("pipe", None, "dp", None),
        P("pipe", None, "dp", None),
        P(None, "pipe", "dp", None),
    )
    return jax.shard_map(
        per_device,
        mesh=mesh,
        in_specs=placed,
        out_specs=P("pipe", None, "dp", None),
        check_vma=False,
    )
```

```python
import functools

import jax
import jax.numpy as jnp
from jax import lax
from jax.experimental import pallas as pl
from jax.experimental.pallas import tpu as pltpu
from jax.sharding import PartitionSpec as P

EPS = 1e-06
LANES = 128
ANY = pl.BlockSpec(memory_space=pl.ANY)
VMEM = pl.BlockSpec(memory_space=pltpu.VMEM)
SMEM = pl.BlockSpec(memory_space=pltpu.SMEM)
LIMIT = 62 * 1024 * 1024
LATE = 32 * 1024 * 1024
COST = pl.CostEstimate(flops=1, bytes_accessed=1, transcendentals=0)
F32 = jnp.float32
BF16 = jnp.bfloat16


def rows_dot(left, right):
    return lax.dot_general(left, right, (((0,), (0,)), ((), ())), preferred_element_type=F32)


def dot_t(left, right):
    return lax.dot_general(left, right, (((1,), (1,)), ((), ())), preferred_element_type=F32)


def dot(left, right):
    return jnp.dot(left, right, preferred_element_type=F32)


def norm_scale(v):
    return lax.rsqrt(jnp.mean(v * v, axis=-1, keepdims=True) + EPS)


def with_scalar(aq, s):
    high = s.astype(BF16).astype(F32)
    at = lax.broadcasted_iota(jnp.int32, (aq.shape[0], LANES), 1)
    tail = jnp.where(at == 0, high, jnp.where(at == 1, s - high, 0.0)).astype(BF16)
    return jnp.concatenate([aq, tail], 1)


def pack_into(out, sources):
    parts, share = out.shape[0], out.shape[3]
    for i, source in enumerate(sources):
        for d in range(parts):
            out[d, i] = source[:, d * share : (d + 1) * share]


def pack_kernel(*refs):
    pack_into(refs[-1], refs[:-1])


def pack(blocks, parts):
    rows, width = blocks[0].shape
    count = len(blocks)
    return pl.pallas_call(
        pack_kernel,
        out_shape=shape(parts, count, rows, width // parts),
        in_specs=[VMEM] * count,
        out_specs=VMEM,
        compiler_params=pltpu.CompilerParams(vmem_limit_bytes=LIMIT),
        cost_estimate=COST,
        name="pack",
    )(*blocks)


def run_copies(pairs, sems):
    copies = [pltpu.make_async_copy(source, target, sems.at[i]) for i, (source, target) in enumerate(pairs)]
    for copy in copies:
        copy.start()
    for copy in copies:
        copy.wait()


def prepare_kernel(down_ref, up_ref, start_ref, packed_ref, x0_ref, y0_ref, x1_ref, sems):
    parts, three, rows, share = packed_ref.shape
    pairs = []
    for i, source in enumerate((down_ref.at[0, 0], start_ref.at[0, 0], down_ref.at[0, 1])):
        for d in range(parts):
            pairs.append((source.at[:, pl.ds(d * share, share)], packed_ref.at[d, i]))
    pairs += [(up_ref.at[0, 0], x0_ref), (start_ref.at[1, 0], y0_ref), (up_ref.at[0, 1], x1_ref)]
    run_copies(pairs, sems)


def prepare(saved_down, saved_up, grad_start, parts):
    rows, width = saved_down.shape[2:]
    share = width // parts
    if share % LANES:
        x0, y0, x1 = saved_up[0, 0], grad_start[1, 0], saved_up[0, 1]
        return pack([saved_down[0, 0], grad_start[0, 0], saved_down[0, 1]], parts), x0, y0, x1
    return pl.pallas_call(
        prepare_kernel,
        out_shape=[shape(parts, 3, rows, share)] + [shape(rows, width)] * 3,
        in_specs=[ANY] * 3,
        out_specs=[VMEM] * 4,
        scratch_shapes=[pltpu.SemaphoreType.DMA((3 * parts + 3,))],
        compiler_params=pltpu.CompilerParams(vmem_limit_bytes=LIMIT),
        cost_estimate=COST,
        name="prepare",
    )(saved_down, saved_up, grad_start)


def shape(*dims, dtype=BF16):
    return jax.ShapeDtypeStruct(dims, dtype)


CHUNKS = 4


def load_chunks(source, buffer, sems):
    chunk = buffer.shape[0] // CHUNKS
    copies = []
    for i in range(CHUNKS):
        part = pl.ds(i * chunk, chunk)
        copies.append(pltpu.make_async_copy(source.at[part], buffer.at[part], sems.at[i]))
    for copy in copies:
        copy.start()
    return copies


def chunked_dot(left, copies, buffer):
    chunk = buffer.shape[0] // CHUNKS
    total = None
    for i, copy in enumerate(copies):
        copy.wait()
        part = dot(left[:, i * chunk : (i + 1) * chunk], buffer[i * chunk : (i + 1) * chunk, :])
        total = part if total is None else total + part
    return total


def latent_gradient(u, c, a, b):
    q = b * (u - c * b * b * jnp.mean(u * c, axis=-1, keepdims=True))
    return (q * a).astype(BF16)


def next_latent(c, a, h, k_ref, c_ref, ab_ref):
    b = norm_scale(c)
    k_ref[...] = (c * b * h).astype(BF16)
    c_ref[...] = c
    at = lax.broadcasted_iota(jnp.int32, (c.shape[0], LANES), 1)
    ab_ref[...] = jnp.where(at == 0, a, b)


def first_kernel(stacked, x_ref, y_ref, w_ref, g_ref, h_ref, *rest):
    rest, (down, up, sem0, sem1) = rest[:-4], rest[-4:]
    copies0 = load_chunks(w_ref.at[0, 0], down, sem0)
    copies1 = load_chunks(w_ref.at[0, 1], up, sem1)
    if stacked:
        x_ref, x1_ref, y_ref = x_ref.at[0, 0], x_ref.at[0, 1], y_ref.at[0, 0]
        z_ref, narrow_ref, k1_ref, c1_ref, ab1_ref = rest
        mine = slice(0, x_ref.shape[0])
    else:
        before_ref, z_ref, narrow_ref = rest
        narrow_ref[: x_ref.shape[0]] = before_ref[...]
        mine = slice(x_ref.shape[0], 2 * x_ref.shape[0])
    rows, width = x_ref.shape
    lat = h_ref.shape[1]
    chunk = width // CHUNKS
    g = g_ref[...].astype(F32)
    h = h_ref[...].astype(F32)
    x = x_ref[...].astype(F32)
    a = norm_scale(x)
    normed = (x * a * g).astype(BF16)
    if stacked:
        x1 = x1_ref[...].astype(F32)
        a1 = norm_scale(x1)
        normed = jnp.concatenate([normed, (x1 * a1 * g).astype(BF16)], 0)
    c = chunked_dot(normed, copies0, down)
    u = chunked_dot(y_ref[...], copies1, up) * h
    if stacked:
        c1 = c[rows:]
        c = c[:rows]
        next_latent(c1, a1, h, k1_ref, c1_ref, ab1_ref)
    b = norm_scale(c)
    narrow_ref[mine, lat + LANES :] = (c * b * h).astype(BF16)
    aq = latent_gradient(u, c, a, b)
    s = a * jnp.sum(aq.astype(F32) * c, axis=-1, keepdims=True) / width
    narrow_ref[mine, : lat + LANES] = with_scalar(aq, s)
    for i in range(CHUNKS):
        cols = slice(i * chunk, (i + 1) * chunk)
        m = dot_t(aq, down[cols, :])
        z = y_ref[:, cols].astype(F32) + m * g[:, cols] - x_ref[:, cols].astype(F32) * s
        z_ref[:, cols] = z.astype(BF16)


def first_step(x, y, weights, g, h, before=None):
    rows, width = x.shape[-2:]
    lat = h.shape[1]
    operands = [x, y, weights, g, h]
    outs = [shape(rows, width)]
    if before is None:
        outs += [shape(rows, 2 * lat + LANES), shape(rows, lat), shape(rows, lat, dtype=F32), shape(rows, LANES, dtype=F32)]
    else:
        outs += [shape(2 * rows, 2 * lat + LANES)]
        operands += [before]
    return pl.pallas_call(
        functools.partial(first_kernel, before is None),
        out_shape=outs,
        in_specs=[VMEM] * 2 + [ANY] + [VMEM] * (len(operands) - 3),
        out_specs=[VMEM] * len(outs),
        scratch_shapes=[pltpu.VMEM((width, lat), BF16)] * 2 + [pltpu.SemaphoreType.DMA((CHUNKS,))] * 2,
        compiler_params=pltpu.CompilerParams(vmem_limit_bytes=LIMIT),
        cost_estimate=COST,
        name="first_step",
    )(*operands)


def latent_kernel(x_ref, w_ref, g_ref, h_ref, k_ref, c_ref, ab_ref, down, sem):
    copies = load_chunks(w_ref.at[0, 0], down, sem)
    x = x_ref[...].astype(F32)
    a = norm_scale(x)
    c = chunked_dot((x * a * g_ref[...].astype(F32)).astype(BF16), copies, down)
    next_latent(c, a, h_ref[...].astype(F32), k_ref, c_ref, ab_ref)


def latent_side(x, weights, g, h):
    rows, width = x.shape
    lat = h.shape[1]
    outs = [shape(rows, lat), shape(rows, lat, dtype=F32), shape(rows, LANES, dtype=F32)]
    return pl.pallas_call(
        latent_kernel,
        out_shape=outs,
        in_specs=[VMEM, ANY, VMEM, VMEM],
        out_specs=[VMEM] * 3,
        scratch_shapes=[pltpu.VMEM((width, lat), BF16), pltpu.SemaphoreType.DMA((CHUNKS,))],
        compiler_params=pltpu.CompilerParams(vmem_limit_bytes=LIMIT),
        cost_estimate=COST,
        name="latent_side",
    )(x, weights, g, h)


def narrow_kernel(y_ref, w_ref, h_ref, k_ref, c_ref, ab_ref, before_ref, narrow_ref, up, sem):
    copies = load_chunks(w_ref.at[0, 1], up, sem)
    rows, width = y_ref.shape
    lat = h_ref.shape[1]
    c, a, b = c_ref[...], ab_ref[:, 0:1], ab_ref[:, 1:2]
    narrow_ref[:rows] = before_ref[...]
    narrow_ref[rows:, lat + LANES :] = k_ref[...]
    aq = latent_gradient(chunked_dot(y_ref[...], copies, up) * h_ref[...].astype(F32), c, a, b)
    s = a * jnp.sum(aq.astype(F32) * c, axis=-1, keepdims=True) / width
    narrow_ref[rows:, : lat + LANES] = with_scalar(aq, s)


def narrow_step(y, weights, h, k, c, ab, before):
    rows, width = y.shape
    lat = h.shape[1]
    return pl.pallas_call(
        narrow_kernel,
        out_shape=shape(2 * rows, 2 * lat + LANES),
        in_specs=[VMEM, ANY] + [VMEM] * 5,
        out_specs=VMEM,
        scratch_shapes=[pltpu.VMEM((width, lat), BF16), pltpu.SemaphoreType.DMA((CHUNKS,))],
        compiler_params=pltpu.CompilerParams(vmem_limit_bytes=LIMIT),
        cost_estimate=COST,
        name="narrow_step",
    )(y, weights, h, k, c, ab, before)


def input_kernel(x_ref, y_ref, w_ref, g_ref, narrow_ref, z_ref, packed_ref, down, sem):
    copies = load_chunks(w_ref.at[0, 0], down, sem)
    rows, width = x_ref.shape
    lat = down.shape[1]
    chunk = width // CHUNKS
    pack_into(packed_ref, [x_ref, y_ref])
    aq = narrow_ref[rows:, :lat]
    s = narrow_ref[rows:, lat : lat + 1].astype(F32) + narrow_ref[rows:, lat + 1 : lat + 2].astype(F32)
    for i, copy in enumerate(copies):
        copy.wait()
        cols = slice(i * chunk, (i + 1) * chunk)
        m = dot_t(aq, down[cols, :])
        z = y_ref[:, cols].astype(F32) + m * g_ref[:, cols].astype(F32) - x_ref[:, cols].astype(F32) * s
        z_ref[:, cols] = z.astype(BF16)


def input_step(x, y, weights, g, narrow, parts):
    rows, width = x.shape
    lat = weights.shape[3]
    return pl.pallas_call(
        input_kernel,
        out_shape=[shape(rows, width), shape(parts, 2, rows, width // parts)],
        in_specs=[VMEM] * 2 + [ANY] + [VMEM] * 2,
        out_specs=[VMEM] * 2,
        scratch_shapes=[pltpu.VMEM((width, lat), BF16), pltpu.SemaphoreType.DMA((CHUNKS,))],
        compiler_params=pltpu.CompilerParams(vmem_limit_bytes=LIMIT),
        cost_estimate=COST,
        name="input_step",
    )(x, y, weights, g, narrow)


def second_kernel(x_ref, y0_ref, y1_ref, w_ref, g_ref, h_ref, c0_ref, ab0_ref, k0_ref, out_ref, packed_ref, down, up, sem0, sem1):
    copies0 = load_chunks(w_ref.at[0, 0], down, sem0)
    copies1 = load_chunks(w_ref.at[0, 1], up, sem1)
    rows, width = x_ref.shape
    lat = h_ref.shape[1]
    pack_into(packed_ref, [x_ref])
    h = h_ref[...].astype(F32)
    x = x_ref[...].astype(F32)
    a = norm_scale(x)
    c = chunked_dot((x * a * g_ref[...].astype(F32)).astype(BF16), copies0, down)
    b = norm_scale(c)
    out_ref[:rows, lat:] = k0_ref[...]
    out_ref[rows:, lat:] = (c * b * h).astype(BF16)
    u = chunked_dot(jnp.concatenate([y0_ref[...], y1_ref[...]], 0), copies1, up) * h
    out_ref[:rows, :lat] = latent_gradient(u[:rows], c0_ref[...], ab0_ref[:, 0:1], ab0_ref[:, 1:2])
    out_ref[rows:, :lat] = latent_gradient(u[rows:], c, a, b)


def second_step(x, y0, y1, weights, g, h, c0, ab0, k0, parts):
    rows, width = x.shape
    lat = h.shape[1]
    return pl.pallas_call(
        second_kernel,
        out_shape=[shape(2 * rows, 2 * lat), shape(parts, 1, rows, width // parts)],
        in_specs=[VMEM] * 3 + [ANY] + [VMEM] * 5,
        out_specs=[VMEM] * 2,
        scratch_shapes=[pltpu.VMEM((width, lat), BF16)] * 2 + [pltpu.SemaphoreType.DMA((CHUNKS,))] * 2,
        compiler_params=pltpu.CompilerParams(vmem_limit_bytes=LIMIT),
        cost_estimate=COST,
        name="second_step",
    )(x, y0, y1, weights, g, h, c0, ab0, k0)


def held_order(parts):
    far = list(range(parts - 2, 0, -2))
    return [0] + far + [p ^ 1 for p in [0] + far]


def gather_pieces(block, axis):
    parts = lax.axis_size(axis)

    def across(held, apart):
        return lax.ppermute(held, axis, [(i, i ^ apart) for i in range(parts)])

    pieces = [block] + [across(block, apart) for apart in range(parts - 2, 0, -2)]
    return pieces + [across(jnp.concatenate(pieces, 0), 1)]


def gather_split(block, axis):
    parts = lax.axis_size(axis)

    def across(held, apart):
        return lax.ppermute(held, axis, [(i, i ^ apart) for i in range(parts)])

    far = [across(block, apart) for apart in range(parts - 2, 0, -2)]
    return [block, *far, across(block, 1), across(jnp.concatenate(far, 0), 1)]


def restore(j, pieces, out):
    parts, rows = out.shape[:2]
    order, at = held_order(parts), 0
    for piece in pieces:
        for i in range(piece.shape[0] // rows):
            out[j ^ order[at]] = piece[i * rows : (i + 1) * rows, :]
            at += 1


def columns_of(x, y, narrow, down, g):
    parts, rows, share = x.shape
    lat = down.shape[3]
    narrow = narrow.reshape(parts * rows, narrow.shape[2])
    s = narrow[:, lat : lat + 1].astype(F32) + narrow[:, lat + 1 : lat + 2].astype(F32)
    m = dot_t(narrow[:, :lat], down[0, 0])
    x = x.reshape(parts * rows, share).astype(F32)
    y = y.reshape(parts * rows, share).astype(F32)
    return (y + m * g[...].astype(F32) - x * s).astype(BF16)


def columns_first_kernel(j_ref, d_ref, down_ref, g_ref, *rest):
    pieces, z_ref, narrow_ref = rest[:-2], rest[-2], rest[-1]
    restore(j_ref[0], pieces, narrow_ref)
    rows = d_ref.shape[2]
    z_ref[...] = columns_of(d_ref[:, 0], d_ref[:, 1], narrow_ref[:, :rows, :], down_ref, g_ref)


def columns_next_kernel(u_ref, down_ref, g_ref, narrow_ref, z_ref):
    rows = u_ref.shape[2]
    z_ref[...] = columns_of(u_ref[:, 0], u_ref[:, 1], narrow_ref[:, rows:, :], down_ref, g_ref)


def columns_first(j, d, down, g, pieces):
    parts, two, rows, share = d.shape
    lat = down.shape[3]
    return pl.pallas_call(
        columns_first_kernel,
        out_shape=[shape(parts * rows, share), shape(parts, *pieces[0].shape)],
        in_specs=[SMEM] + [VMEM] * (3 + len(pieces)),
        out_specs=[VMEM, VMEM],
        compiler_params=pltpu.CompilerParams(vmem_limit_bytes=LATE),
        cost_estimate=COST,
        name="columns_first",
    )(j, d, down, g, *pieces)


def columns_next(u, down, g, narrow):
    parts, two, rows, share = u.shape
    lat = down.shape[3]
    return pl.pallas_call(
        columns_next_kernel,
        out_shape=shape(parts * rows, share),
        in_specs=[VMEM] * 4,
        out_specs=VMEM,
        compiler_params=pltpu.CompilerParams(vmem_limit_bytes=LATE),
        cost_estimate=COST,
        name="columns_next",
    )(u, down, g, narrow)


def first_terms_kernel(d_ref, u_ref, first_ref, out_ref):
    parts, three, rows, share = d_ref.shape
    lat = out_ref.shape[2]
    total = parts * rows
    for at, start in ((0, 0), (1, lat + LANES)):
        down = first_ref[:, :rows, start : start + lat].reshape(total, lat)
        up = first_ref[:, rows:, start : start + lat].reshape(total, lat)
        both = rows_dot(d_ref[:, at].reshape(total, share), down)
        out_ref[at] = (both + rows_dot(u_ref[:, at].reshape(total, share), up)).astype(BF16)


def first_terms(d, u, first, lat):
    share = d.shape[3]
    return pl.pallas_call(
        first_terms_kernel,
        out_shape=shape(2, share, lat),
        in_specs=[VMEM] * 3,
        out_specs=VMEM,
        compiler_params=pltpu.CompilerParams(vmem_limit_bytes=LATE),
        cost_estimate=COST,
        name="first_terms",
    )(d, u, first)


def terms_kernel(j_ref, d_ref, x1_ref, y1d_ref, y1u_ref, part_ref, g_ref, *rest):
    pieces, out_ref, second_ref = rest[:-2], rest[-2], rest[-1]
    parts, three, rows, share = d_ref.shape
    lat = second_ref.shape[2] // 2
    total = parts * rows
    restore(j_ref[0], pieces, second_ref)

    def half(i, start):
        return second_ref[:, i * rows : (i + 1) * rows, start : start + lat].reshape(total, lat)

    first = part_ref[0].astype(F32) + rows_dot(d_ref[:, 2].reshape(total, share), half(0, 0))
    first += rows_dot(x1_ref[:, 0].reshape(total, share), half(1, 0))
    out_ref[0, 0] = (first * g_ref[...].astype(F32)).astype(BF16)
    second = part_ref[1].astype(F32) + rows_dot(y1d_ref[...], half(0, lat))
    second += rows_dot(y1u_ref[...], half(1, lat))
    out_ref[0, 1] = second.astype(BF16)


def terms(j, d, x1, y1d, y1u, part, g, pieces):
    parts, three, rows, share = d.shape
    narrow = pieces[0].shape
    return pl.pallas_call(
        terms_kernel,
        out_shape=shape(1, 2, share, narrow[1] // 2),
        in_specs=[SMEM] + [VMEM] * (6 + len(pieces)),
        out_specs=VMEM,
        scratch_shapes=[pltpu.VMEM((parts,) + narrow, BF16)],
        compiler_params=pltpu.CompilerParams(vmem_limit_bytes=LATE),
        cost_estimate=COST,
        name="terms",
    )(j, d, x1, y1d, y1u, part, g, *pieces)


def per_device(weights, gain_model, gain_latent, saved_down, saved_up, grad_start):
    ranks = lax.axis_size("pipe")
    replicas = lax.axis_size("dp")
    j = lax.axis_index("dp")
    share = weights.shape[2] // replicas
    own_down = lax.dynamic_slice(weights, (0, 0, j * share, 0), (1, 1, share, weights.shape[3]))
    own_g = lax.dynamic_slice_in_dim(gain_model, j * share, share, 1)

    def mirror(block):
        return lax.ppermute(block, "pipe", [(i, ranks - 1 - i) for i in range(ranks)])

    def to_before(block):
        return lax.ppermute(block, "pipe", [(i + 1, i) for i in range(ranks - 1)])

    def exchange(blocks):
        return lax.all_to_all(blocks, "dp", 0, 0, tiled=True)

    packed, x0u, y0u, x1u = prepare(saved_down, saved_up, grad_start, replicas)
    packed, x0u, y0u, x1u, saved_down, grad_start = lax.optimization_barrier((packed, x0u, y0u, x1u, saved_down, grad_start))
    x0u, y0u, x1u = mirror(x0u), mirror(y0u), mirror(x1u)
    d_s = exchange(packed)
    z0d, before, k1d, c1d, ab1d = first_step(saved_down, grad_start, weights, gain_model, gain_latent)
    y1d = to_before(z0d)
    column_g = own_g.reshape(share, 1)
    x0u, before, own_down, own_g, column_g = lax.optimization_barrier((x0u, before, own_down, own_g, column_g))
    k0u, c0u, ab0u = latent_side(x0u, weights, gain_model, gain_latent)
    narrow = narrow_step(y0u, weights, gain_latent, k0u, c0u, ab0u, before)
    first_pieces = gather_pieces(narrow, "dp")
    far = len(first_pieces) - 1
    z0u, u_packed = input_step(x0u, y0u, weights, gain_model, narrow, replicas)
    y1u = to_before(z0u)
    u_packed, x1u, y1d, d_s, *first_pieces[1:far] = lax.optimization_barrier((u_packed, x1u, y1d, d_s, *first_pieces[1:far]))
    u_s = exchange(u_packed)
    second, x1_packed = second_step(x1u, y1d, y1u, weights, gain_model, gain_latent, c1d, ab1d, k1d, replicas)
    second_pieces = gather_split(second, "dp")
    z0d_s, first = columns_first(j[None], d_s, own_down, own_g, first_pieces)
    y1d_s = to_before(z0d_s)
    z0u_s = columns_next(u_s, own_down, own_g, first)
    z0u_s, x1_packed, *second_pieces[1 : far + 1] = lax.optimization_barrier((z0u_s, x1_packed, *second_pieces[1 : far + 1]))
    x1_s = exchange(x1_packed)
    y1u_s = to_before(z0u_s)
    part = first_terms(d_s, u_s, first, gain_latent.shape[1])
    return terms(j[None], d_s, x1_s, y1d_s, y1u_s, part, column_g, second_pieces)


def solution(mesh):
    placed = (
        P("pipe", None, None, None),
        P("pipe", None),
        P("pipe", None),
        P("pipe", None, "dp", None),
        P("pipe", None, "dp", None),
        P(None, "pipe", "dp", None),
    )
    return jax.shard_map(
        per_device,
        mesh=mesh,
        in_specs=placed,
        out_specs=P("pipe", None, "dp", None),
        check_vma=False,
    )
```
